512 devices in a mesh: lat: 32 (over z_hi, x, core), lon: 16 (over y, z_lo).
Axes of the slice: x: 4, y: 4, z: 16 (z_hi: 4, z_lo: 4; z = z_hi * 4 + z_lo), core: 2. Of those that a mesh axis runs over, the one named last changes fastest.
Arguments:
- state_field: float32 [384, 384, 256], P('lat', 'lon'), may hold values from -6 to 6
- cotangent: bfloat16 [384, 384, 256], P('lat', 'lon'), may hold values from -6 to 6
- depthwise: float32 [49, 256], replicated, may hold values from -0.875 to 0.875
- norm_gain: float32 [256], replicated, may hold values from 0.4 to 1.6
- w_in: bfloat16 [256, 1024], replicated, may hold values from -0.375 to 0.375
- w_out: bfloat16 [1024, 256], replicated, may hold values from -0.1875 to 0.1875
Outputs:
- block_out: bfloat16 [384, 384, 256], P('lat', 'lon')
- grad_input: bfloat16 [384, 384, 256], P('lat', 'lon')
- weight_grads: float32 [1024, 512], P(('lat', 'lon'))
- grad_depthwise: float32 [49, 256], replicated
- grad_gain: float32 [256], replicated
The draws below stay inside these ranges and needn't reach their ends.
All inputs are finite; a program needn't handle non-finite values.
Results may differ from the reference program's by a relative error of at most 0.0052.
Values sent between devices are 32-bit elements; how exact they have to be, the bound alone decides.
No kernel may reach another device: no remote copies, remote signals or barrier semaphores. Data moves between devices by JAX's collectives and lax.ppermute only.
A program may use at most 64 MiB of HBM per device.

```python
import math
import jax
import jax.numpy as jnp
from jax import lax

C = 256
FF = 1024
NLAT = 384
NLON = 384


def level_of(stream_key, dims, split, least, high):
    gain, own = 1.0, jax.random.fold_in(stream_key, 6)
    for position, shards_of in split:
        draws = jnp.exp(jax.random.uniform(jax.random.fold_in(own, position), (shards_of,), jnp.float32, least / len(split), high / len(split)))
        gain = gain * jnp.repeat(draws, dims[position] // shards_of).reshape([-1 if axis == position else 1 for axis in range(len(dims))])
    return gain


def bell_draw(own_key, dims, spread, reach, pieces=(), kind=jnp.bfloat16):
    gain = level_of(own_key, dims, pieces, -0.22, 0.18) if pieces else 1.0
    entries = jax.random.normal(own_key, dims, jnp.float32) * spread * gain
    return jnp.minimum(jnp.maximum(entries, -reach), reach).astype(kind)


def setup_inputs(seed: int = 0) -> dict:
    seeds = jax.random.split(jax.random.key(seed), 7)
    return {
        "state_field": bell_draw(seeds[0], (NLAT, NLON, C), 1.0, 6.0, ((0, 32), (1, 16)), jnp.float32),
        "cotangent": bell_draw(seeds[1], (NLAT, NLON, C), 1.0, 6.0, ((0, 32), (1, 16))),
        "depthwise": bell_draw(seeds[2], (49, C), 49 ** -0.5, 0.875, (), jnp.float32),
        "norm_gain": jnp.clip(1.0 + 0.12 * jax.random.normal(seeds[3], (C,), jnp.float32), 0.4, 1.6),
        "w_in": bell_draw(seeds[4], (C, FF), C ** -0.5, 0.375),
        "w_out": bell_draw(seeds[5], (FF, C), FF ** -0.5, 0.1875),
    }


def gelu_value(values):
    return 0.5 * values * (1.0 + lax.erf(values * 0.7071067811865476))

def gelu_slope(values):
    return 0.5 * (1.0 + lax.erf(values * 0.7071067811865476)) + values * jnp.exp(-0.5 * values * values) * 0.3989422804014327

def layer_norm(convolved, norm_gain):
    average = lax.optimization_barrier(jnp.mean(convolved, axis=-1, keepdims=True))
    centred_raw = convolved - average
    variance = lax.optimization_barrier(jnp.mean(centred_raw * centred_raw, axis=-1, keepdims=True))
    inv_std = 1.0 / jnp.sqrt(variance + 1e-06)
    centred = centred_raw * inv_std
    normed = (centred * norm_gain).astype(jnp.bfloat16)
    return (normed, centred, inv_std)

def extend(state_field, half_turn):
    top_rows = jnp.roll(jnp.flip(state_field[:3], 0), -half_turn, axis=1)
    bottom_rows = jnp.roll(jnp.flip(state_field[-3:], 0), -half_turn, axis=1)
    tall = jnp.concatenate([top_rows, state_field, bottom_rows], 0)
    return jnp.concatenate([tall[:, -3:], tall, tall[:, :3]], 1)

def apply_taps(extended, depthwise, lat_rows, lon_cols):
    running = jnp.zeros((lat_rows, lon_cols, extended.shape[2]), jnp.float32)
    for row_off in range(7):
        for col_off in range(7):
            running = running + depthwise[7 * row_off + col_off] * extended[row_off:row_off + lat_rows, col_off:col_off + lon_cols]
    return running

def adjoint_taps(grad_conv, depthwise, lat_rows, lon_cols):
    padded = jnp.pad(grad_conv, ((6, 6), (6, 6), (0, 0)))
    running = jnp.zeros((lat_rows + 6, lon_cols + 6, grad_conv.shape[2]), jnp.float32)
    for row_off in range(7):
        for col_off in range(7):
            running = running + depthwise[7 * row_off + col_off] * padded[6 - row_off:12 - row_off + lat_rows, 6 - col_off:12 - col_off + lon_cols]
    return running

def fold(tap_grid, half_turn):
    interior = tap_grid[:, 3:-3]
    interior = interior.at[:, :3].add(tap_grid[:, -3:]).at[:, -3:].add(tap_grid[:, :3])
    inner = interior[3:-3]
    inner = inner.at[:3].add(jnp.flip(jnp.roll(interior[:3], half_turn, axis=1), 0))
    inner = inner.at[-3:].add(jnp.flip(jnp.roll(interior[-3:], half_turn, axis=1), 0))
    return inner

def reference(state_field, cotangent, depthwise, norm_gain, w_in, w_out):
    lat_rows, lon_cols, channels = state_field.shape
    unit_count = w_in.shape[1]
    half_turn = lon_cols // 2
    grad_scale = 1.0 / math.sqrt(lat_rows * lon_cols)
    extended = extend(state_field, half_turn)
    convolved = apply_taps(extended, depthwise, lat_rows, lon_cols)

    def row_step(running, inputs):
        unit_sum, gain_sum = running
        conv_row, field_row, cot_row = inputs
        normed, centred, inv_std = layer_norm(conv_row, norm_gain)
        pre_act = jnp.dot(normed, w_in, preferred_element_type=jnp.float32)
        hidden = gelu_value(pre_act).astype(jnp.bfloat16)
        branch = jnp.dot(hidden, w_out, preferred_element_type=jnp.float32)
        out_row = (field_row + branch).astype(jnp.bfloat16)
        grad_hidden = jnp.dot(cot_row, w_out.T, preferred_element_type=jnp.float32)
        grad_pre = (grad_hidden * gelu_slope(pre_act)).astype(jnp.bfloat16)
        grad_normed = jnp.dot(grad_pre, w_in.T, preferred_element_type=jnp.float32)
        scaled_grad = grad_normed * norm_gain
        grad_conv = inv_std * (scaled_grad - lax.optimization_barrier(jnp.mean(scaled_grad, axis=-1, keepdims=True)) - centred * lax.optimization_barrier(jnp.mean(scaled_grad * centred, axis=-1, keepdims=True)))
        weight_terms = jnp.concatenate([jnp.dot(grad_pre.T, normed, preferred_element_type=jnp.float32), jnp.dot(hidden.T, cot_row, preferred_element_type=jnp.float32)], 1)
        gain_terms = lax.optimization_barrier(jnp.sum(grad_normed * centred, axis=0))
        return ((unit_sum + weight_terms, gain_sum + gain_terms), (out_row, grad_conv))
    initial = (jnp.zeros((unit_count, 2 * channels), jnp.float32), jnp.zeros((channels,), jnp.float32))
    (unit_sum, gain_sum), (block_out, grad_conv) = lax.scan(row_step, initial, (convolved, state_field, cotangent))
    tap_grid = adjoint_taps(grad_conv, depthwise, lat_rows, lon_cols)
    grad_input = (cotangent.astype(jnp.float32) + fold(tap_grid, half_turn)).astype(jnp.bfloat16)
    tap_list = []
    for row_off in range(7):
        for col_off in range(7):
            tap_list.append(lax.optimization_barrier(jnp.sum(extended[row_off:row_off + lat_rows, col_off:col_off + lon_cols] * grad_conv, axis=(0, 1))))
    grad_depthwise = jnp.stack(tap_list, 0) * grad_scale
    return (block_out, grad_input, unit_sum * grad_scale, grad_depthwise, gain_sum * grad_scale)
```

```python
import math

import jax
import jax.numpy as jnp
from jax import lax
from jax.sharding import Mesh, PartitionSpec as P

AXES = ("zh", "x", "core", "y", "zl")
SIZES = (4, 4, 2, 4, 4)
LAT = 32
LON = 16


def gelu_value(values):
    return 0.5 * values * (1.0 + lax.erf(values * 0.7071067811865476))


def gelu_slope(values):
    return (
        0.5 * (1.0 + lax.erf(values * 0.7071067811865476))
        + values * jnp.exp(-0.5 * values * values) * 0.3989422804014327
    )


def layer_norm(convolved, norm_gain):
    average = jnp.mean(convolved, axis=-1, keepdims=True)
    centred_raw = convolved - average
    variance = jnp.mean(centred_raw * centred_raw, axis=-1, keepdims=True)
    inv_std = 1.0 / jnp.sqrt(variance + 1e-06)
    centred = centred_raw * inv_std
    normed = (centred * norm_gain).astype(jnp.bfloat16)
    return (normed, centred, inv_std)


def lat_lon():
    lat = (lax.axis_index("zh") * 4 + lax.axis_index("x")) * 2 + lax.axis_index("core")
    return lat, lax.axis_index("y") * 4 + lax.axis_index("zl")


def row_pairs():
    first, second = [], []
    for lat in range(LAT):
        for lon in range(LON):
            here = lat * LON + lon
            first.append((here, (lat ^ 1) * LON + lon))
            if lat == 0 or lat == LAT - 1:
                peer = lat * LON + (lon + LON // 2) % LON
            else:
                peer = (lat - 1 if lat % 2 == 0 else lat + 1) * LON + lon
            second.append((here, peer))
    return first, second


def column_pairs():
    right, left = [], []
    for lat in range(LAT):
        for lon in range(LON):
            here = lat * LON + lon
            right.append((here, lat * LON + (lon + 1) % LON))
            left.append((here, lat * LON + (lon - 1) % LON))
    return right, left


def halo(values):
    lat, _ = lat_lon()
    even = lat % 2 == 0
    pole = (lat == 0) | (lat == LAT - 1)
    head, tail = values[:3], values[-3:]
    first, second = row_pairs()
    outer = jnp.where(even, head, tail)
    outer = jnp.where(pole, jnp.flip(outer, 0), outer)
    got_first = lax.ppermute(jnp.where(even, tail, head), AXES, first)
    got_second = lax.ppermute(outer, AXES, second)
    above = jnp.where(even, got_second, got_first)
    below = jnp.where(even, got_first, got_second)
    tall = jnp.concatenate([above, values, below], 0)
    right, left = column_pairs()
    before = lax.ppermute(tall[:, -3:], AXES, right)
    after = lax.ppermute(tall[:, :3], AXES, left)
    return jnp.concatenate([before, tall, after], 1)


def apply_taps(extended, depthwise, height, breadth):
    running = jnp.zeros((height, breadth, extended.shape[2]), jnp.float32)
    for row_off in range(7):
        for col_off in range(7):
            running = (
                running
                + depthwise[7 * row_off + col_off]
                * extended[row_off : row_off + height, col_off : col_off + breadth]
            )
    return running


def adjoint_taps(wide, depthwise, height, breadth):
    lat, _ = lat_lon()
    taps = depthwise.reshape(7, 7, -1)
    flipped = jnp.flip(taps, 0)
    upper = jnp.where(lat == 0, flipped, taps)
    lower = jnp.where(lat == LAT - 1, flipped, taps)
    rows = wide.shape[0]
    running = jnp.zeros((height, breadth, wide.shape[2]), jnp.float32)
    for row_off in range(7):
        start = 6 - row_off
        for col_off in range(7):
            weight = []
            for i in range(height):
                r = i + start
                weight.append(
                    (upper if r < 3 else lower if r >= rows - 3 else taps)[row_off, col_off]
                )
            weight = jnp.stack(weight, 0)[:, None, :]
            running = running + weight * wide[start : start + height, 6 - col_off : 6 - col_off + breadth]
    return running


def tap_sums(extended, grad_conv, height, breadth):
    tap_list = []
    for row_off in range(7):
        for col_off in range(7):
            tap_list.append(
                jnp.sum(
                    extended[row_off : row_off + height, col_off : col_off + breadth] * grad_conv,
                    axis=(0, 1),
                )
            )
    return tap_list


def body(state_field, cotangent, depthwise, norm_gain, w_in, w_out):
    height, breadth, channels = state_field.shape
    units = w_in.shape[1]
    cell_count = height * breadth
    grad_scale = 1.0 / math.sqrt(cell_count * LAT * LON)
    extended = halo(state_field)
    convolved = apply_taps(extended, depthwise, height, breadth)
    normed, centred, inv_std = layer_norm(convolved.reshape(cell_count, channels), norm_gain)
    pre_act = jnp.dot(normed, w_in, preferred_element_type=jnp.float32)
    hidden = gelu_value(pre_act).astype(jnp.bfloat16)
    branch = jnp.dot(hidden, w_out, preferred_element_type=jnp.float32)
    block_out = (
        (state_field.reshape(cell_count, channels) + branch)
        .astype(jnp.bfloat16)
        .reshape(height, breadth, channels)
    )
    cot_flat = cotangent.reshape(cell_count, channels)
    grad_hidden = lax.dot_general(
        cot_flat, w_out, (((1,), (1,)), ((), ())), preferred_element_type=jnp.float32
    )
    grad_pre = (grad_hidden * gelu_slope(pre_act)).astype(jnp.bfloat16)
    grad_normed = lax.dot_general(
        grad_pre, w_in, (((1,), (1,)), ((), ())), preferred_element_type=jnp.float32
    )
    scaled_grad = grad_normed * norm_gain
    grad_conv = inv_std * (
        scaled_grad
        - jnp.mean(scaled_grad, axis=-1, keepdims=True)
        - centred * jnp.mean(scaled_grad * centred, axis=-1, keepdims=True)
    )
    gain_local = jnp.sum(grad_normed * centred, axis=0)
    left_part = jnp.einsum("pf,pc->fc", grad_pre, normed, preferred_element_type=jnp.float32)
    right_part = jnp.einsum("pf,pc->fc", hidden, cot_flat, preferred_element_type=jnp.float32)
    local = jnp.concatenate([left_part, right_part], 1)
    local = local.reshape(4, 4, 2, 4, 8, 4, 128).transpose(2, 1, 3, 5, 0, 4, 6)
    local = local.reshape(2, 16, 128, 128)
    core = lax.axis_index("core")
    theirs = lax.ppermute(jnp.where(core == 0, local[1], local[0]), "core", [(0, 1), (1, 0)])
    mine = jnp.where(core == 0, local[0], local[1]) + theirs

    grad_conv = grad_conv.reshape(height, breadth, channels)
    taps = jnp.stack(
        tap_sums(extended, grad_conv, height, breadth)
        + [gain_local]
        + [jnp.zeros_like(gain_local)] * 14,
        0,
    ).reshape(16, 8, 128)
    wide = halo(grad_conv)
    grad_input = (
        cotangent.astype(jnp.float32) + adjoint_taps(wide, depthwise, height, breadth)
    ).astype(jnp.bfloat16)

    plane = lax.all_to_all(
        jnp.concatenate([mine, taps], 1), ("x", "y"), split_axis=0, concat_axis=0, tiled=True
    ).sum(0)
    rest = plane[:128].reshape(4, 4, 4, 2, 128).transpose(1, 2, 0, 3, 4).reshape(16, 8, 128)
    column = lax.all_to_all(
        jnp.concatenate([rest, jnp.broadcast_to(plane[128:], (16, 8, 128))], 1),
        ("zh", "zl"),
        split_axis=0,
        concat_axis=0,
        tiled=True,
    ).sum(0)
    weight_grads = column[:8].reshape(4, 2, 128).transpose(1, 0, 2).reshape(2, 512) * grad_scale
    shared = lax.all_to_all(
        jnp.broadcast_to(column[8:], (32, 8, 128)),
        ("x", "core", "y"),
        split_axis=0,
        concat_axis=0,
        tiled=True,
    )
    totals = shared.reshape(4, 2, 4, 8, 128).sum(1).reshape(64, 256) * grad_scale
    return (block_out, grad_input, weight_grads, totals[:49], totals[49])


def solution(mesh):
    split = Mesh(mesh.devices.reshape(SIZES), AXES)
    cells = P(("zh", "x", "core"), ("y", "zl"), None)
    return jax.shard_map(
        body,
        mesh=split,
        in_specs=(cells, cells, P(), P(), P(), P()),
        out_specs=(cells, cells, P(AXES, None), P(), P()),
        check_vma=False,
    )
```

```python
import functools
import math

import jax
import jax.numpy as jnp
from jax import lax
from jax.experimental import pallas as pl
from jax.experimental.pallas import tpu as pltpu
from jax.sharding import Mesh, PartitionSpec as P

AXES = ("zh", "x", "core", "y", "zl")
SIZES = (4, 4, 2, 4, 4)
LAT = 32
LON = 16


def lat_lon():
    lat = (lax.axis_index("zh") * 4 + lax.axis_index("x")) * 2 + lax.axis_index("core")
    return lat, lax.axis_index("y") * 4 + lax.axis_index("zl")


def row_pairs():
    first, second = [], []
    for lat in range(LAT):
        for lon in range(LON):
            here = lat * LON + lon
            first.append((here, (lat ^ 1) * LON + lon))
            if lat == 0 or lat == LAT - 1:
                peer = lat * LON + (lon + LON // 2) % LON
            else:
                peer = (lat - 1 if lat % 2 == 0 else lat + 1) * LON + lon
            second.append((here, peer))
    return first, second


def column_pairs():
    right, left = [], []
    for lat in range(LAT):
        for lon in range(LON):
            here = lat * LON + lon
            right.append((here, lat * LON + (lon + 1) % LON))
            left.append((here, lat * LON + (lon - 1) % LON))
    return right, left


H = 12
W = 24
C = 256
FF = 1024
CELLS = H * W
PARAMS = pltpu.CompilerParams(vmem_limit_bytes=48 * 1024 * 1024)


def gelu_parts(values):
    phi = 0.5 * (1.0 + lax.erf(values * 0.7071067811865476))
    slope = phi + values * jnp.exp(-0.5 * values * values) * 0.3989422804014327
    return values * phi, slope


def fill(wide_ref, above, below, centre, before, after):
    wide_ref[0:3, 8 : 8 + W, :] = above[...]
    wide_ref[3 : 3 + H, 8 : 8 + W, :] = centre[...]
    wide_ref[3 + H :, 8 : 8 + W, :] = below[...]
    wide_ref[:, 5:8, :] = before[...]
    wide_ref[:, 8 + W : 11 + W, :] = after[...]


def window(wide_ref, row, col, lanes):
    return wide_ref[row, 5 + col : 5 + col + W, lanes]


def convolve(wide_ref, weight, lanes):
    total = [None] * H
    for col in range(7):
        for row in range(H + 6):
            part = window(wide_ref, row, col, lanes)
            for tap in range(7):
                out = row - tap
                if 0 <= out < H:
                    term = weight(row, tap, col, lanes) * part
                    total[out] = term if total[out] is None else total[out] + term
    return total


def forward_kernel(
    core_ref, above, below, state, before, after, cot, taps, gain, w_in, w_out,
    block_out, grad_conv, mine, theirs, gain_sum,
    wide, conv, hidden, grad_pre,
):
    fill(wide, above, below, state, before, after)
    for half in range(2):
        lanes = slice(128 * half, 128 * half + 128)
        total = convolve(
            wide, lambda row, tap, col, ln: taps[7 * tap + col : 7 * tap + col + 1, ln], lanes
        )
        for out in range(H):
            conv[W * out : W * out + W, lanes] = total[out]
    values = conv[...]
    centred = values - jnp.mean(values, axis=-1, keepdims=True)
    variance = jnp.mean(centred * centred, axis=-1, keepdims=True)
    inv_std = 1.0 / jnp.sqrt(variance + 1e-06)
    centred = centred * inv_std
    conv[...] = centred
    normed = (centred * gain[...]).astype(jnp.bfloat16)
    cotangent = cot[...]
    branch = state[...].reshape(CELLS, C)
    grad_normed = jnp.zeros((CELLS, C), jnp.float32)
    for part in range(4):
        cols = slice(256 * part, 256 * part + 256)
        pre_act = jnp.dot(normed, w_in[:, cols], preferred_element_type=jnp.float32)
        grad_hidden = lax.dot_general(
            cotangent, w_out[cols, :], (((1,), (1,)), ((), ())), preferred_element_type=jnp.float32
        )
        value, slope = gelu_parts(pre_act)
        hid = value.astype(jnp.bfloat16)
        gpre = (grad_hidden * slope).astype(jnp.bfloat16)
        hidden[:, cols] = hid
        grad_pre[:, cols] = gpre
    core = core_ref[0]
    for part in range(4):
        cols = slice(256 * part, 256 * part + 256)
        hid = hidden[:, cols]
        gpre = grad_pre[:, cols]
        branch = branch + jnp.dot(hid, w_out[cols, :], preferred_element_type=jnp.float32)
        grad_normed = grad_normed + lax.dot_general(
            gpre, w_in[:, cols], (((1,), (1,)), ((), ())), preferred_element_type=jnp.float32
        )
        for side, (left, right) in enumerate(((gpre, normed), (hid, cotangent))):
            product = lax.dot_general(
                left, right, (((0,), (0,)), ((), ())), preferred_element_type=jnp.float32
            )
            for x in range(4):
                for run in range(2):
                    lanes = slice(128 * run, 128 * run + 128)
                    ours = product[64 * x : 64 * x + 32, lanes]
                    other = product[64 * x + 32 : 64 * x + 64, lanes]
                    keep = jnp.where(core == 0, ours, other)
                    send = jnp.where(core == 0, other, ours)
                    row = 32 * (2 * side + run) + 8 * part
                    mine[4 * x : 4 * x + 4, row : row + 8, :] = keep.reshape(4, 8, 128)
                    theirs[4 * x : 4 * x + 4, row : row + 8, :] = send.reshape(4, 8, 128)
    block_out[...] = branch.astype(jnp.bfloat16)
    centred = conv[...]
    scaled = grad_normed * gain[...]
    grad = inv_std * (
        scaled
        - jnp.mean(scaled, axis=-1, keepdims=True)
        - centred * jnp.mean(scaled * centred, axis=-1, keepdims=True)
    )
    gain_sum[...] = jnp.sum(grad_normed * centred, axis=0, keepdims=True)
    grad_conv[...] = grad.reshape(H, W, C)


def tap_kernel(above, below, state, before, after, grad_conv, gain_sum, out, wide):
    fill(wide, above, below, state, before, after)
    for half in range(2):
        lanes = slice(128 * half, 128 * half + 128)
        grad = [grad_conv[row, :, lanes] for row in range(H)]
        for col in range(7):
            total = [jnp.zeros((8, 128), jnp.float32)] * 7
            for row in range(H + 6):
                part = window(wide, row, col, lanes)
                for tap in range(7):
                    if 0 <= row - tap < H:
                        term = part * grad[row - tap]
                        total[tap] = total[tap] + ((term[0:8] + term[8:16]) + term[16:24])
            for tap in range(7):
                place = 64 * half + 7 * tap + col
                out[place : place + 1, :] = jnp.sum(total[tap], axis=0, keepdims=True)
        out[64 * half + 49 : 64 * half + 50, :] = gain_sum[:, lanes]
        out[64 * half + 50 : 64 * half + 64, :] = jnp.zeros((14, 128), jnp.float32)


def adjoint_kernel(lat_ref, above, below, grad_conv, before, after, cot, taps, out, wide, rim, grad):
    fill(wide, above, below, grad_conv, before, after)
    lat = lat_ref[0]
    for tap in range(7):
        here = taps[7 * tap : 7 * tap + 7, :]
        turned = taps[7 * (6 - tap) : 7 * (6 - tap) + 7, :]
        rim[0, tap, 0:7, :] = jnp.where(lat == 0, turned, here)
        rim[1, tap, 0:7, :] = jnp.where(lat == LAT - 1, turned, here)

    def weight(row, tap, col, lanes):
        if row < 3:
            return rim[0, 6 - tap, 6 - col : 7 - col, lanes]
        if row >= H + 3:
            return rim[1, 6 - tap, 6 - col : 7 - col, lanes]
        place = 7 * (6 - tap) + 6 - col
        return taps[place : place + 1, lanes]

    for half in range(2):
        lanes = slice(128 * half, 128 * half + 128)
        total = convolve(wide, weight, lanes)
        for row in range(H):
            grad[W * row : W * row + W, lanes] = total[row]
    out[...] = (cot[...].astype(jnp.float32) + grad[...]).astype(jnp.bfloat16)


def join_kernel(mine, theirs, taps, out):
    out[:, 0:128, :] = mine[...] + theirs[...]
    out[:, 128:136, :] = taps[...].reshape(16, 8, 128)


def plane_kernel(got, out):
    total = got[0]
    for peer in range(1, 16):
        total = total + got[peer]
    for zh in range(4):
        for zl in range(4):
            place = 4 * zh + zl
            for run in range(4):
                row = 32 * run + 8 * zh + 2 * zl
                out[place, 2 * run : 2 * run + 2, :] = total[row : row + 2]
            out[place, 8:16, :] = total[128:136]


def column_kernel(scale, got, weight_grads, shared):
    total = got[0]
    for peer in range(1, 16):
        total = total + got[peer]
    total = total * scale
    for run in range(4):
        weight_grads[:, 128 * run : 128 * run + 128] = total[2 * run : 2 * run + 2]
    for peer in range(32):
        shared[peer] = total[8:16]


def total_kernel(got, taps, gain):
    for half in range(2):
        rows = []
        for place in range(8 * half, 8 * half + 8):
            x, y = place // 4, place % 4
            rows.append(got[8 * x + y] + got[8 * x + 4 + y])
        table = jnp.concatenate(rows, 0)
        taps[:, 128 * half : 128 * half + 128] = table[0:49]
        gain[:, 128 * half : 128 * half + 128] = table[49:50]


def call(kernel, out, *args, scratch=(), scalars=0):
    vmem = pl.BlockSpec(memory_space=pltpu.VMEM)
    smem = pl.BlockSpec(memory_space=pltpu.SMEM)
    many = isinstance(out, list)
    return pl.pallas_call(
        kernel,
        out_shape=[jax.ShapeDtypeStruct(s, d) for s, d in (out if many else [out])],
        in_specs=[smem] * scalars + [vmem] * (len(args) - scalars),
        out_specs=[vmem] * (len(out) if many else 1),
        scratch_shapes=[pltpu.VMEM(s, d) for s, d in scratch],
        compiler_params=PARAMS,
    )(*args)


F32 = jnp.float32
BF16 = jnp.bfloat16
WIDE = ((H + 6, 40, C), F32)


def halo(values):
    lat, _ = lat_lon()
    even = lat % 2 == 0
    pole = (lat == 0) | (lat == LAT - 1)
    head, tail = values[:3], values[-3:]
    first, second = row_pairs()
    outer = jnp.where(even, head, tail)
    outer = jnp.where(pole, jnp.flip(outer, 0), outer)
    got_first = lax.ppermute(jnp.where(even, tail, head), AXES, first)
    got_second = lax.ppermute(outer, AXES, second)
    above = jnp.where(even, got_second, got_first)
    below = jnp.where(even, got_first, got_second)
    right, left = column_pairs()
    edge = jnp.concatenate([above[:, -3:], values[:, -3:], below[:, -3:]], 0)
    before = lax.ppermute(edge, AXES, right)
    edge = jnp.concatenate([above[:, :3], values[:, :3], below[:, :3]], 0)
    after = lax.ppermute(edge, AXES, left)
    return above, below, values, before, after


def body(state_field, cotangent, depthwise, norm_gain, w_in, w_out):
    grad_scale = 1.0 / math.sqrt(CELLS * LAT * LON)
    lat, _ = lat_lon()
    lat = lat.astype(jnp.int32).reshape(1)
    core = lax.axis_index("core").astype(jnp.int32).reshape(1)
    cot = cotangent.reshape(CELLS, C)
    pieces = halo(state_field)
    block_out, grad_conv, mine, theirs, gain_sum = call(
        forward_kernel,
        [
            ((CELLS, C), BF16),
            ((H, W, C), F32),
            ((16, 128, 128), F32),
            ((16, 128, 128), F32),
            ((1, C), F32),
        ],
        core, *pieces, cot, depthwise, norm_gain.reshape(1, C), w_in, w_out,
        scratch=[WIDE, ((CELLS, C), F32), ((CELLS, FF), BF16), ((CELLS, FF), BF16)],
        scalars=1,
    )
    theirs = lax.ppermute(theirs, "core", [(0, 1), (1, 0)])
    (taps,) = call(tap_kernel, ((128, 128), F32), *pieces, grad_conv, gain_sum, scratch=[WIDE])
    grad_pieces = halo(grad_conv)
    (joined,) = call(join_kernel, ((16, 136, 128), F32), mine, theirs, taps)
    plane = lax.all_to_all(joined, ("x", "y"), split_axis=0, concat_axis=0, tiled=True)
    (spread,) = call(plane_kernel, ((16, 16, 128), F32), plane)
    column = lax.all_to_all(spread, ("zh", "zl"), split_axis=0, concat_axis=0, tiled=True)
    weight_grads, shared = call(
        functools.partial(column_kernel, grad_scale), [((2, 512), F32), ((32, 8, 128), F32)], column
    )
    shared = lax.all_to_all(shared, ("x", "core", "y"), split_axis=0, concat_axis=0, tiled=True)
    (grad_input,) = call(
        adjoint_kernel,
        ((CELLS, C), BF16),
        lat, *grad_pieces, cot, depthwise,
        scratch=[WIDE, ((2, 7, 8, C), F32), ((CELLS, C), F32)],
        scalars=1,
    )
    tap_total, gain_total = call(total_kernel, [((49, C), F32), ((1, C), F32)], shared)
    return (
        block_out.reshape(H, W, C),
        grad_input.reshape(H, W, C),
        weight_grads,
        tap_total,
        gain_total.reshape(C),
    )


def solution(mesh):
    split = Mesh(mesh.devices.reshape(SIZES), AXES)
    cells = P(("zh", "x", "core"), ("y", "zl"), None)
    return jax.shard_map(
        body,
        mesh=split,
        in_specs=(cells, cells, P(), P(), P(), P()),
        out_specs=(cells, cells, P(AXES, None), P(), P()),
        check_vma=False,
    )
```

```python
import functools
import math

import jax
import jax.numpy as jnp
from jax import lax
from jax.experimental import pallas as pl
from jax.experimental.pallas import tpu as pltpu
from jax.sharding import Mesh, PartitionSpec as P

AXES = ("zh", "x", "core", "y", "zl")
SIZES = (4, 4, 2, 4, 4)
LAT = 32
LON = 16


def lat_lon():
    lat = (lax.axis_index("zh") * 4 + lax.axis_index("x")) * 2 + lax.axis_index("core")
    return lat, lax.axis_index("y") * 4 + lax.axis_index("zl")


def row_pairs():
    first, second = [], []
    for lat in range(LAT):
        for lon in range(LON):
            here = lat * LON + lon
            first.append((here, (lat ^ 1) * LON + lon))
            if lat == 0 or lat == LAT - 1:
                peer = lat * LON + (lon + LON // 2) % LON
            else:
                peer = (lat - 1 if lat % 2 == 0 else lat + 1) * LON + lon
            second.append((here, peer))
    return first, second


def column_pairs():
    right, left = [], []
    for lat in range(LAT):
        for lon in range(LON):
            here = lat * LON + lon
            right.append((here, lat * LON + (lon + 1) % LON))
            left.append((here, lat * LON + (lon - 1) % LON))
    return right, left


H = 12
W = 24
C = 256
FF = 1024
V = 32
CELLS = H * W
WIDE_CELLS = H * V
EDGE = 6 * (H + 6) + 3 * H
PARAMS = pltpu.CompilerParams(vmem_limit_bytes=20 * 1024 * 1024)


def gelu_parts(values):
    phi = 0.5 * (1.0 + lax.erf(values * 0.7071067811865476))
    slope = phi + values * jnp.exp(-0.5 * values * values) * 0.3989422804014327
    return values * phi, slope


def window(wide_ref, row, col, width, lanes):
    return wide_ref[row, col : col + width, lanes]


def convolve(wide_ref, weight, base, width, lanes):
    total = [None] * H
    for col in range(7):
        for row in range(H + 6):
            part = window(wide_ref, row, base + col, width, lanes)
            for tap in range(7):
                out = row - tap
                if 0 <= out < H:
                    term = weight(row, tap, col, lanes) * part
                    total[out] = term if total[out] is None else total[out] + term
    return total


def own_edge_kernel(
    state_hbm, cot_hbm, gain_hbm, w_in_hbm, w_out_hbm,
    to_right, to_left, gain, w_in, w_out,
    state, cot, full, sem,
):
    fetches = [
        pltpu.make_async_copy(source, target, sem.at[i])
        for i, (source, target) in enumerate(
            (
                (state_hbm, state),
                (cot_hbm, cot),
                (gain_hbm, gain),
                (w_in_hbm, w_in),
                (w_out_hbm, w_out),
            )
        )
    ]
    for fetch in fetches:
        fetch.start()
    fetches[0].wait()
    for row in range(H):
        to_right[6 * row : 6 * row + 6, :] = state[row, W - 6 : W, :]
        to_left[6 * row : 6 * row + 6, :] = state[row, 0:6, :]
    fetches[1].wait()
    full[...] = cot[...].astype(jnp.float32)
    for row in range(H):
        place = 6 * H + 3 * row
        to_right[place : place + 3, :] = full[W * row + W - 3 : W * row + W, :]
        to_left[place : place + 3, :] = full[W * row : W * row + 3, :]
    for fetch in fetches[2:]:
        fetch.wait()


def edge_kernel(even_ref, first, second, own_right, own_left, above, below, to_right, to_left):
    even = even_ref[0] == 1
    above[...] = jnp.where(even, second[...], first[...])
    below[...] = jnp.where(even, first[...], second[...])
    to_right[0 : 9 * H, :] = own_right[...]
    to_left[0 : 9 * H, :] = own_left[...]
    for row in range(3):
        for place, ref in ((9 * H, above), (9 * H + 18, below)):
            spot = place + 6 * row
            to_right[spot : spot + 6, :] = ref[row, W - 6 : W, :]
            to_left[spot : spot + 6, :] = ref[row, 0:6, :]


def source_row(above, state, below, row):
    if row < 3:
        return above[row], 9 * H + 6 * row
    if row < H + 3:
        return state[row - 3], 6 * (row - 3)
    return below[row - H - 3], 9 * H + 18 + 6 * (row - H - 3)


def forward_kernel(
    core_ref, above, below, state, before, after, cot, taps, gain, w_in, w_out,
    mine, theirs, hidden, grad_pre, centred_out, inv_out,
    wide, conv, cot_all,
):
    wide[:, 32:40, :] = jnp.zeros((H + 6, 8, C), jnp.float32)
    for row in range(H + 6):
        centre, spot = source_row(above, state, below, row)
        wide[row, 8 : 8 + W, :] = centre
        wide[row, 2:8, :] = before[spot : spot + 6, :]
        wide[row, 8 + W : 14 + W, :] = after[spot : spot + 6, :]
    cot_all[:, 24:32, :] = jnp.zeros((H, 8, C), jnp.float32)
    own = cot[...].astype(jnp.float32)
    for row in range(H):
        place = 6 * H + 3 * row
        cot_all[row, 0:3, :] = before[place : place + 3, :]
        cot_all[row, 3 : 3 + W, :] = own[W * row : W * row + W]
        cot_all[row, 3 + W : 6 + W, :] = after[place : place + 3, :]
    for half in range(2):
        lanes = slice(128 * half, 128 * half + 128)
        total = convolve(
            wide, lambda row, tap, col, ln: taps[7 * tap + col : 7 * tap + col + 1, ln], 2, V, lanes
        )
        for out in range(H):
            conv[V * out : V * out + V, lanes] = total[out]
    values = conv[...]
    centred = values - jnp.mean(values, axis=-1, keepdims=True)
    variance = jnp.mean(centred * centred, axis=-1, keepdims=True)
    inv_std = 1.0 / jnp.sqrt(variance + 1e-06)
    centred = centred * inv_std
    centred_out[...] = centred
    inv_out[...] = jnp.broadcast_to(inv_std, (WIDE_CELLS, 128))
    place = lax.broadcasted_iota(jnp.int32, (H, V, C), 1).reshape(WIDE_CELLS, C)
    inside = (place >= 3) & (place < 3 + W)
    normed = centred * gain[...]
    own_normed = jnp.where(inside, normed, 0.0).astype(jnp.bfloat16)
    normed = normed.astype(jnp.bfloat16)
    cotangent = cot_all[...].reshape(WIDE_CELLS, C)
    own_cot = jnp.where(inside, cotangent, 0.0).astype(jnp.bfloat16)
    cotangent = cotangent.astype(jnp.bfloat16)
    core = core_ref[0]
    for part in range(4):
        cols = slice(256 * part, 256 * part + 256)
        pre_act = jnp.dot(normed, w_in[:, cols], preferred_element_type=jnp.float32)
        grad_hidden = lax.dot_general(
            cotangent, w_out[cols, :], (((1,), (1,)), ((), ())), preferred_element_type=jnp.float32
        )
        value, slope = gelu_parts(pre_act)
        hidden[:, cols] = value.astype(jnp.bfloat16)
        grad_pre[:, cols] = (grad_hidden * slope).astype(jnp.bfloat16)
    for part in range(4):
        cols = slice(256 * part, 256 * part + 256)
        for side, (left, right) in enumerate(
            ((grad_pre[:, cols], own_normed), (hidden[:, cols], own_cot))
        ):
            product = lax.dot_general(
                left, right, (((0,), (0,)), ((), ())), preferred_element_type=jnp.float32
            )
            for x in range(4):
                for run in range(2):
                    lanes = slice(128 * run, 128 * run + 128)
                    ours = product[64 * x : 64 * x + 32, lanes]
                    other = product[64 * x + 32 : 64 * x + 64, lanes]
                    keep = jnp.where(core == 0, ours, other)
                    send = jnp.where(core == 0, other, ours)
                    row = 32 * (2 * side + run) + 8 * part
                    mine[4 * x : 4 * x + 4, row : row + 8, :] = keep.reshape(4, 8, 128)
                    theirs[4 * x : 4 * x + 4, row : row + 8, :] = send.reshape(4, 8, 128)


def backward_kernel(
    above, below, state, before, after, gain, w_in, grad_pre, centred_in, inv_in,
    grad_conv, out,
    wide,
):
    for row in range(H + 6):
        centre, spot = source_row(above, state, below, row)
        wide[row, 8 : 8 + W, :] = centre
        wide[row, 5:8, :] = before[spot + 3 : spot + 6, :]
        wide[row, 8 + W : 11 + W, :] = after[spot : spot + 3, :]
    grad_normed = lax.dot_general(
        grad_pre[...], w_in[...], (((1,), (1,)), ((), ())), preferred_element_type=jnp.float32
    )
    centred = centred_in[...]
    inv_std = inv_in[...][:, 0:1]
    scaled = grad_normed * gain[...]
    grad = inv_std * (
        scaled
        - jnp.mean(scaled, axis=-1, keepdims=True)
        - centred * jnp.mean(scaled * centred, axis=-1, keepdims=True)
    )
    place = lax.broadcasted_iota(jnp.int32, (H, V, C), 1).reshape(WIDE_CELLS, C)
    inside = (place >= 3) & (place < 3 + W)
    gain_sum = jnp.sum(jnp.where(inside, grad_normed * centred, 0.0), axis=0, keepdims=True)
    grad_conv[...] = grad.reshape(H, V, C)
    for half in range(2):
        lanes = slice(128 * half, 128 * half + 128)
        grads = [grad_conv[row, 3 : 3 + W, lanes] for row in range(H)]
        for col in range(7):
            total = [jnp.zeros((8, 128), jnp.float32)] * 7
            for row in range(H + 6):
                part = window(wide, row, 5 + col, W, lanes)
                for tap in range(7):
                    if 0 <= row - tap < H:
                        term = part * grads[row - tap]
                        total[tap] = total[tap] + ((term[0:8] + term[8:16]) + term[16:24])
            for tap in range(7):
                spot = 64 * half + 7 * tap + col
                out[spot : spot + 1, :] = jnp.sum(total[tap], axis=0, keepdims=True)
        out[64 * half + 49 : 64 * half + 50, :] = gain_sum[:, lanes]
        out[64 * half + 50 : 64 * half + 64, :] = jnp.zeros((14, 128), jnp.float32)


def adjoint_kernel(
    where_ref, first, second, grad_conv, cot, taps, state, hidden, w_out,
    out, block_out,
    wide, rim, grad, branch_ref,
):
    branch = jnp.dot(hidden[...], w_out[...], preferred_element_type=jnp.float32)
    branch_ref[...] = branch.reshape(H, V, C)
    block_out[...] = (state[...] + branch_ref[:, 3 : 3 + W, :]).reshape(CELLS, C).astype(jnp.bfloat16)
    lat = where_ref[0]
    even = where_ref[1] == 1
    wide[0:3] = jnp.where(even, second[...], first[...])
    wide[3 : 3 + H] = grad_conv[...]
    wide[3 + H :] = jnp.where(even, first[...], second[...])
    for tap in range(7):
        here = taps[7 * tap : 7 * tap + 7, :]
        turned = taps[7 * (6 - tap) : 7 * (6 - tap) + 7, :]
        rim[0, tap, 0:7, :] = jnp.where(lat == 0, turned, here)
        rim[1, tap, 0:7, :] = jnp.where(lat == LAT - 1, turned, here)

    def weight(row, tap, col, lanes):
        if row < 3:
            return rim[0, 6 - tap, 6 - col : 7 - col, lanes]
        if row >= H + 3:
            return rim[1, 6 - tap, 6 - col : 7 - col, lanes]
        place = 7 * (6 - tap) + 6 - col
        return taps[place : place + 1, lanes]

    for half in range(2):
        lanes = slice(128 * half, 128 * half + 128)
        total = convolve(wide, weight, 0, W, lanes)
        for row in range(H):
            grad[W * row : W * row + W, lanes] = total[row]
    out[...] = (cot[...].astype(jnp.float32) + grad[...]).astype(jnp.bfloat16)


def join_kernel(mine, theirs, taps, out):
    out[:, 0:128, :] = mine[...] + theirs[...]
    out[:, 128:136, :] = taps[...].reshape(16, 8, 128)


def plane_kernel(got, out):
    total = got[0]
    for peer in range(1, 16):
        total = total + got[peer]
    for zh in range(4):
        for zl in range(4):
            place = 4 * zh + zl
            for run in range(4):
                row = 32 * run + 8 * zh + 2 * zl
                out[place, 2 * run : 2 * run + 2, :] = total[row : row + 2]
            out[place, 8:16, :] = total[128:136]


def column_kernel(scale, got, weight_grads, shared):
    total = got[0]
    for peer in range(1, 16):
        total = total + got[peer]
    total = total * scale
    for run in range(4):
        weight_grads[:, 128 * run : 128 * run + 128] = total[2 * run : 2 * run + 2]
    for peer in range(32):
        shared[peer] = total[8:16]


def total_kernel(got, taps, gain):
    for half in range(2):
        rows = []
        for place in range(8 * half, 8 * half + 8):
            x, y = place // 4, place % 4
            rows.append(got[8 * x + y] + got[8 * x + 4 + y])
        table = jnp.concatenate(rows, 0)
        taps[:, 128 * half : 128 * half + 128] = table[0:49]
        gain[:, 128 * half : 128 * half + 128] = table[49:50]


def call(kernel, out, *args, scratch=(), scalars=0, held=()):
    vmem = pl.BlockSpec(memory_space=pltpu.VMEM)
    smem = pl.BlockSpec(memory_space=pltpu.SMEM)
    anywhere = pl.BlockSpec(memory_space=pltpu.HBM)
    return pl.pallas_call(
        kernel,
        out_shape=[jax.ShapeDtypeStruct(s, d) for s, d in out],
        in_specs=[
            smem if i < scalars else anywhere if i in held else vmem for i in range(len(args))
        ],
        out_specs=[vmem] * len(out),
        scratch_shapes=[pltpu.VMEM(*s) if isinstance(s, tuple) else s for s in scratch],
        compiler_params=PARAMS,
    )(*args)


F32 = jnp.float32
BF16 = jnp.bfloat16
WIDE = ((H + 6, 40, C), F32)


def row_exchange(values, even, pole):
    head, tail = values[:3], values[-3:]
    first, second = row_pairs()
    outer = jnp.where(even, head, tail)
    outer = jnp.where(pole, jnp.flip(outer, 0), outer)
    got_first = lax.ppermute(jnp.where(even, tail, head), AXES, first)
    got_second = lax.ppermute(outer, AXES, second)
    return got_first, got_second


def body(state_field, cotangent, depthwise, norm_gain, w_in, w_out):
    grad_scale = 1.0 / math.sqrt(CELLS * LAT * LON)
    lat, _ = lat_lon()
    lat = lat.astype(jnp.int32)
    even = lat % 2 == 0
    pole = (lat == 0) | (lat == LAT - 1)
    parity = even.astype(jnp.int32)
    core = lax.axis_index("core").astype(jnp.int32).reshape(1)
    cot = cotangent.reshape(CELLS, C)
    gain = norm_gain.reshape(1, C)
    *own_edges, gain, w_in, w_out = call(
        own_edge_kernel,
        [
            ((9 * H, C), F32),
            ((9 * H, C), F32),
            ((1, C), F32),
            ((C, FF), BF16),
            ((FF, C), BF16),
        ],
        state_field, cot, gain, w_in, w_out,
        scratch=[
            ((H, W, C), F32),
            ((CELLS, C), BF16),
            ((CELLS, C), F32),
            pltpu.SemaphoreType.DMA((5,)),
        ],
        held=(0, 1, 2, 3, 4),
    )
    rows = row_exchange(state_field, even, pole)
    above, below, to_right, to_left = call(
        edge_kernel,
        [((3, W, C), F32), ((3, W, C), F32), ((EDGE, C), F32), ((EDGE, C), F32)],
        parity.reshape(1), *rows, *own_edges,
        scalars=1,
    )
    right, left = column_pairs()
    before = lax.ppermute(to_right, AXES, right)
    after = lax.ppermute(to_left, AXES, left)
    pieces = (above, below, state_field, before, after)
    mine, theirs, hidden, grad_pre, centred, inv_std = call(
        forward_kernel,
        [
            ((16, 128, 128), F32),
            ((16, 128, 128), F32),
            ((WIDE_CELLS, FF), BF16),
            ((WIDE_CELLS, FF), BF16),
            ((WIDE_CELLS, C), F32),
            ((WIDE_CELLS, 128), F32),
        ],
        core, *pieces, cot, depthwise, gain, w_in, w_out,
        scratch=[
            WIDE,
            ((WIDE_CELLS, C), F32),
            ((H, V, C), F32),
        ],
        scalars=1,
    )
    theirs = lax.ppermute(theirs, "core", [(0, 1), (1, 0)])
    grad_conv, taps = call(
        backward_kernel,
        [((H, V, C), F32), ((128, 128), F32)],
        *pieces, gain, w_in, grad_pre, centred, inv_std,
        scratch=[WIDE],
    )
    (joined,) = call(join_kernel, [((16, 136, 128), F32)], mine, theirs, taps)
    plane = lax.all_to_all(joined, ("x", "y"), split_axis=0, concat_axis=0, tiled=True)
    grad_rows = row_exchange(grad_conv, even, pole)
    plane, grad_rows = lax.optimization_barrier((plane, grad_rows))
    (spread,) = call(plane_kernel, [((16, 16, 128), F32)], plane)
    column = lax.all_to_all(spread, ("zh", "zl"), split_axis=0, concat_axis=0, tiled=True)
    grad_input, block_out = call(
        adjoint_kernel,
        [((CELLS, C), BF16), ((CELLS, C), BF16)],
        jnp.stack([lat, parity]), *grad_rows, grad_conv, cot, depthwise, state_field, hidden, w_out,
        scratch=[
            ((H + 6, V, C), F32),
            ((2, 7, 8, C), F32),
            ((CELLS, C), F32),
            ((H, V, C), F32),
        ],
        scalars=1,
    )
    column, grad_input = lax.optimization_barrier((column, grad_input))
    weight_grads, shared = call(
        functools.partial(column_kernel, grad_scale), [((2, 512), F32), ((32, 8, 128), F32)], column
    )
    shared = lax.all_to_all(shared, ("x", "core", "y"), split_axis=0, concat_axis=0, tiled=True)
    tap_total, gain_total = call(total_kernel, [((49, C), F32), ((1, C), F32)], shared)
    return (
        block_out.reshape(H, W, C),
        grad_input.reshape(H, W, C),
        weight_grads,
        tap_total,
        gain_total.reshape(C),
    )


def solution(mesh):
    split = Mesh(mesh.devices.reshape(SIZES), AXES)
    cells = P(("zh", "x", "core"), ("y", "zl"), None)
    return jax.shard_map(
        body,
        mesh=split,
        in_specs=(cells, cells, P(), P(), P(), P()),
        out_specs=(cells, cells, P(AXES, None), P(), P()),
        check_vma=False,
    )
```

```python
import functools
import math

import jax
import jax.numpy as jnp
from jax import lax
from jax.experimental import pallas as pl
from jax.experimental.pallas import tpu as pltpu
from jax.sharding import Mesh, PartitionSpec as P

AXES = ("zh", "x", "core", "y", "zl")
SIZES = (4, 4, 2, 4, 4)
LAT = 32
LON = 16


def lat_lon():
    lat = (lax.axis_index("zh") * 4 + lax.axis_index("x")) * 2 + lax.axis_index("core")
    return lat, lax.axis_index("y") * 4 + lax.axis_index("zl")


def row_pairs():
    first, second = [], []
    for lat in range(LAT):
        for lon in range(LON):
            here = lat * LON + lon
            first.append((here, (lat ^ 1) * LON + lon))
            if lat == 0 or lat == LAT - 1:
                peer = lat * LON + (lon + LON // 2) % LON
            else:
                peer = (lat - 1 if lat % 2 == 0 else lat + 1) * LON + lon
            second.append((here, peer))
    return first, second


def column_pairs():
    right, left = [], []
    for lat in range(LAT):
        for lon in range(LON):
            here = lat * LON + lon
            right.append((here, lat * LON + (lon + 1) % LON))
            left.append((here, lat * LON + (lon - 1) % LON))
    return right, left


H = 12
W = 24
C = 256
FF = 1024
V = 32
CELLS = H * W
M = 16
HALF_CELLS = H * M
EDGE = 6 * (H + 6) + 3 * H
PARAMS = pltpu.CompilerParams(vmem_limit_bytes=20 * 1024 * 1024)


def gelu_parts(values):
    phi = 0.5 * (1.0 + lax.erf(values * 0.7071067811865476))
    slope = phi + values * jnp.exp(-0.5 * values * values) * 0.3989422804014327
    return values * phi, slope


def window(wide_ref, row, col, width, lanes):
    return wide_ref[row, col : col + width, lanes]


def convolve(wide_ref, weight, base, width, lanes):
    total = [None] * H
    for col in range(7):
        for row in range(H + 6):
            part = window(wide_ref, row, base + col, width, lanes)
            for tap in range(7):
                out = row - tap
                if 0 <= out < H:
                    term = weight(row, tap, col, lanes) * part
                    total[out] = term if total[out] is None else total[out] + term
    return total


def own_edge_kernel(
    state_hbm, cot_hbm, gain_hbm, w_in_hbm, w_out_hbm,
    to_right, to_left, gain, w_in, w_out,
    state, cot, full, sem,
):
    fetches = [
        pltpu.make_async_copy(source, target, sem.at[i])
        for i, (source, target) in enumerate(
            (
                (state_hbm, state),
                (cot_hbm, cot),
                (gain_hbm, gain),
                (w_in_hbm, w_in),
                (w_out_hbm, w_out),
            )
        )
    ]
    for fetch in fetches:
        fetch.start()
    fetches[0].wait()
    for row in range(H):
        to_right[6 * row : 6 * row + 6, :] = state[row, W - 6 : W, :]
        to_left[6 * row : 6 * row + 6, :] = state[row, 0:6, :]
    fetches[1].wait()
    full[...] = cot[...].astype(jnp.float32)
    for row in range(H):
        place = 6 * H + 3 * row
        to_right[place : place + 3, :] = full[W * row + W - 3 : W * row + W, :]
        to_left[place : place + 3, :] = full[W * row : W * row + 3, :]
    for fetch in fetches[2:]:
        fetch.wait()


def edge_kernel(even_ref, first, second, own_right, own_left, above, below, to_right, to_left):
    even = even_ref[0] == 1
    above[...] = jnp.where(even, second[...], first[...])
    below[...] = jnp.where(even, first[...], second[...])
    to_right[0 : 9 * H, :] = own_right[...]
    to_left[0 : 9 * H, :] = own_left[...]
    for row in range(3):
        for place, ref in ((9 * H, above), (9 * H + 18, below)):
            spot = place + 6 * row
            to_right[spot : spot + 6, :] = ref[row, W - 6 : W, :]
            to_left[spot : spot + 6, :] = ref[row, 0:6, :]


def source_row(above, state, below, row):
    if row < 3:
        return above[row], 9 * H + 6 * row
    if row < H + 3:
        return state[row - 3], 6 * (row - 3)
    return below[row - H - 3], 9 * H + 18 + 6 * (row - H - 3)


def normalise(values):
    centred = values - jnp.mean(values, axis=-1, keepdims=True)
    variance = jnp.mean(centred * centred, axis=-1, keepdims=True)
    inv_std = 1.0 / jnp.sqrt(variance + 1e-06)
    return centred * inv_std, inv_std


def activate(normed, cotangent, w_in, w_out, hidden, grad_pre):
    for part in range(4):
        cols = slice(256 * part, 256 * part + 256)
        pre_act = jnp.dot(normed, w_in[:, cols], preferred_element_type=jnp.float32)
        grad_hidden = lax.dot_general(
            cotangent, w_out[cols, :], (((1,), (1,)), ((), ())), preferred_element_type=jnp.float32
        )
        value, slope = gelu_parts(pre_act)
        hidden[:, cols] = value.astype(jnp.bfloat16)
        grad_pre[:, cols] = (grad_hidden * slope).astype(jnp.bfloat16)


def weight_products(core, grad_pre, normed, hidden, cotangent, mine, theirs, before):
    for part in range(4):
        cols = slice(256 * part, 256 * part + 256)
        for side, (left, right) in enumerate(((grad_pre[:, cols], normed), (hidden[:, cols], cotangent))):
            product = lax.dot_general(
                left, right, (((0,), (0,)), ((), ())), preferred_element_type=jnp.float32
            )
            for x in range(4):
                for run in range(2):
                    lanes = slice(128 * run, 128 * run + 128)
                    ours = product[64 * x : 64 * x + 32, lanes]
                    other = product[64 * x + 32 : 64 * x + 64, lanes]
                    keep = jnp.where(core == 0, ours, other).reshape(4, 8, 128)
                    send = jnp.where(core == 0, other, ours).reshape(4, 8, 128)
                    row = 32 * (2 * side + run) + 8 * part
                    places = (slice(4 * x, 4 * x + 4), slice(row, row + 8), slice(None))
                    if before is not None:
                        keep = keep + before[0][places]
                        send = send + before[1][places]
                    mine[places] = keep
                    theirs[places] = send


def norm_gradient(grad_pre, w_in, gain, centred, inv_std):
    grad_normed = lax.dot_general(
        grad_pre, w_in, (((1,), (1,)), ((), ())), preferred_element_type=jnp.float32
    )
    scaled = grad_normed * gain
    grad = inv_std * (
        scaled
        - jnp.mean(scaled, axis=-1, keepdims=True)
        - centred * jnp.mean(scaled * centred, axis=-1, keepdims=True)
    )
    return grad, grad_normed * centred


def tap_sums(wide, starts, grads, out, gain_sum, before):
    for half in range(2):
        lanes = slice(128 * half, 128 * half + 128)
        pieces = grads(lanes)
        for col in range(7):
            total = [jnp.zeros((8, 128), jnp.float32)] * 7
            for row in range(H + 6):
                for start, piece in zip(starts, pieces):
                    width = piece[0].shape[0]
                    part = window(wide, row, start + col, width, lanes)
                    for tap in range(7):
                        if 0 <= row - tap < H:
                            term = part * piece[row - tap]
                            for tile in range(0, width, 8):
                                total[tap] = total[tap] + term[tile : tile + 8]
            for tap in range(7):
                spot = 64 * half + 7 * tap + col
                value = jnp.sum(total[tap], axis=0, keepdims=True)
                out[spot : spot + 1, :] = (
                    value if before is None else value + before[spot : spot + 1, :]
                )
        spot = 64 * half + 49
        value = gain_sum[:, lanes]
        out[spot : spot + 1, :] = value if before is None else value + before[spot : spot + 1, :]
        out[spot + 1 : spot + 15, :] = jnp.zeros((14, 128), jnp.float32)


def tap_weight(taps):
    return lambda row, tap, col, lanes: taps[7 * tap + col : 7 * tap + col + 1, lanes]


def middle_kernel(
    core_ref, above, below, state, cot, taps, gain, w_in, w_out,
    mine, theirs, hidden, grad_out, tap_out,
    wide, conv, full, grad_pre,
):
    wide[0:3] = above[...]
    wide[3 : 3 + H] = state[...]
    wide[3 + H :] = below[...]
    full[...] = cot[...].astype(jnp.float32).reshape(H, W, C)
    for half in range(2):
        lanes = slice(128 * half, 128 * half + 128)
        total = convolve(wide, tap_weight(taps), 2, M, lanes)
        for out in range(H):
            conv[M * out : M * out + M, lanes] = total[out]
    centred, inv_std = normalise(conv[...])
    normed = (centred * gain[...]).astype(jnp.bfloat16)
    cotangent = full[:, 5 : 5 + M, :].reshape(HALF_CELLS, C).astype(jnp.bfloat16)
    activate(normed, cotangent, w_in, w_out, hidden, grad_pre)
    weight_products(core_ref[0], grad_pre, normed, hidden, cotangent, mine, theirs, None)
    grad, gains = norm_gradient(grad_pre[...], w_in[...], gain[...], centred, inv_std)
    grad_out[...] = grad.reshape(H, M, C)
    tap_sums(
        wide,
        (2,),
        lambda lanes: [[grad_out[row, :, lanes] for row in range(H)]],
        tap_out,
        jnp.sum(gains, axis=0, keepdims=True),
        None,
    )


def fill(wide, above, below, state, before, after):
    wide[:, 32:40, :] = jnp.zeros((H + 6, 8, C), jnp.float32)
    for row in range(H + 6):
        centre, spot = source_row(above, state, below, row)
        wide[row, 8 : 8 + W, :] = centre
        wide[row, 2:8, :] = before[spot : spot + 6, :]
        wide[row, 8 + W : 14 + W, :] = after[spot : spot + 6, :]


def forward_kernel(
    core_ref, above, below, state, before, after, cot, taps, gain, w_in, w_out, mine_in, theirs_in,
    mine, theirs, hidden, grad_pre, centred_out, inv_out,
    wide, conv, cot_all,
):
    fill(wide, above, below, state, before, after)
    cot_all[:, 8:16, :] = jnp.zeros((H, 8, C), jnp.float32)
    own = cot[...].astype(jnp.float32)
    for row in range(H):
        place = 6 * H + 3 * row
        cot_all[row, 0:3, :] = before[place : place + 3, :]
        cot_all[row, 3:8, :] = own[W * row : W * row + 5]
        cot_all[row, 8:11, :] = own[W * row + W - 3 : W * row + W]
        cot_all[row, 11:14, :] = after[place : place + 3, :]
    for half in range(2):
        lanes = slice(128 * half, 128 * half + 128)
        for side, base in enumerate((2, 26)):
            total = convolve(wide, tap_weight(taps), base, 8, lanes)
            for out in range(H):
                spot = M * out + 8 * side
                conv[spot : spot + 8, lanes] = total[out]
    centred, inv_std = normalise(conv[...])
    centred_out[...] = centred
    inv_out[...] = jnp.broadcast_to(inv_std, (HALF_CELLS, 128))
    inside = is_inside()
    normed = centred * gain[...]
    own_normed = jnp.where(inside, normed, 0.0).astype(jnp.bfloat16)
    normed = normed.astype(jnp.bfloat16)
    cotangent = cot_all[...].reshape(HALF_CELLS, C)
    own_cot = jnp.where(inside, cotangent, 0.0).astype(jnp.bfloat16)
    cotangent = cotangent.astype(jnp.bfloat16)
    activate(normed, cotangent, w_in, w_out, hidden, grad_pre)
    weight_products(
        core_ref[0], grad_pre, own_normed, hidden, own_cot, mine, theirs, (mine_in, theirs_in)
    )


def is_inside():
    place = lax.broadcasted_iota(jnp.int32, (H, M, C), 1).reshape(HALF_CELLS, C)
    return (place >= 3) & (place < 11)


def backward_kernel(
    above, below, state, before, after, gain, w_in, grad_pre, centred_in, inv_in, grad_mid, tap_mid,
    grad_conv, out,
    wide, own_grad,
):
    fill(wide, above, below, state, before, after)
    grad, gains = norm_gradient(grad_pre[...], w_in[...], gain[...], centred_in[...], inv_in[...][:, 0:1])
    inside = is_inside()
    own_grad[...] = jnp.where(inside, grad, 0.0).reshape(H, M, C)
    grad = grad.reshape(H, M, C)
    grad_conv[:, 0:8, :] = grad[:, 0:8]
    grad_conv[:, 8:24, :] = grad_mid[...]
    grad_conv[:, 24:32, :] = grad[:, 8:16]
    tap_sums(
        wide,
        (2, 26),
        lambda lanes: [
            [own_grad[row, spot : spot + 8, lanes] for row in range(H)] for spot in (0, 8)
        ],
        out,
        jnp.sum(jnp.where(inside, gains, 0.0), axis=0, keepdims=True),
        tap_mid,
    )


def adjoint_kernel(
    where_ref, first, second, grad_conv, cot, taps, state, middle, outer, w_out,
    out, block_out,
    wide, rim, grad, branch_ref,
):
    branch = jnp.dot(middle[...], w_out[...], preferred_element_type=jnp.float32)
    branch_ref[:, 8:24, :] = branch.reshape(H, M, C)
    branch = jnp.dot(outer[...], w_out[...], preferred_element_type=jnp.float32).reshape(H, M, C)
    branch_ref[:, 0:8, :] = branch[:, 0:8]
    branch_ref[:, 24:32, :] = branch[:, 8:16]
    block_out[...] = (state[...] + branch_ref[:, 3 : 3 + W, :]).reshape(CELLS, C).astype(jnp.bfloat16)
    lat = where_ref[0]
    even = where_ref[1] == 1
    wide[0:3] = jnp.where(even, second[...], first[...])
    wide[3 : 3 + H] = grad_conv[...]
    wide[3 + H :] = jnp.where(even, first[...], second[...])
    for tap in range(7):
        here = taps[7 * tap : 7 * tap + 7, :]
        turned = taps[7 * (6 - tap) : 7 * (6 - tap) + 7, :]
        rim[0, tap, 0:7, :] = jnp.where(lat == 0, turned, here)
        rim[1, tap, 0:7, :] = jnp.where(lat == LAT - 1, turned, here)

    def weight(row, tap, col, lanes):
        if row < 3:
            return rim[0, 6 - tap, 6 - col : 7 - col, lanes]
        if row >= H + 3:
            return rim[1, 6 - tap, 6 - col : 7 - col, lanes]
        place = 7 * (6 - tap) + 6 - col
        return taps[place : place + 1, lanes]

    for half in range(2):
        lanes = slice(128 * half, 128 * half + 128)
        total = convolve(wide, weight, 0, W, lanes)
        for row in range(H):
            grad[W * row : W * row + W, lanes] = total[row]
    out[...] = (cot[...].astype(jnp.float32) + grad[...]).astype(jnp.bfloat16)


def join_kernel(mine, theirs, taps, out):
    out[:, 0:128, :] = mine[...] + theirs[...]
    out[:, 128:136, :] = taps[...].reshape(16, 8, 128)


def plane_kernel(got, out):
    total = got[0]
    for peer in range(1, 16):
        total = total + got[peer]
    for zh in range(4):
        for zl in range(4):
            place = 4 * zh + zl
            for run in range(4):
                row = 32 * run + 8 * zh + 2 * zl
                out[place, 2 * run : 2 * run + 2, :] = total[row : row + 2]
            out[place, 8:16, :] = total[128:136]


def column_kernel(scale, got, weight_grads, shared):
    total = got[0]
    for peer in range(1, 16):
        total = total + got[peer]
    total = total * scale
    for run in range(4):
        weight_grads[:, 128 * run : 128 * run + 128] = total[2 * run : 2 * run + 2]
    for peer in range(32):
        shared[peer] = total[8:16]


def total_kernel(got, taps, gain):
    for half in range(2):
        rows = []
        for place in range(8 * half, 8 * half + 8):
            x, y = place // 4, place % 4
            rows.append(got[8 * x + y] + got[8 * x + 4 + y])
        table = jnp.concatenate(rows, 0)
        taps[:, 128 * half : 128 * half + 128] = table[0:49]
        gain[:, 128 * half : 128 * half + 128] = table[49:50]


def call(kernel, out, *args, scratch=(), scalars=0, held=()):
    vmem = pl.BlockSpec(memory_space=pltpu.VMEM)
    smem = pl.BlockSpec(memory_space=pltpu.SMEM)
    anywhere = pl.BlockSpec(memory_space=pltpu.HBM)
    return pl.pallas_call(
        kernel,
        out_shape=[jax.ShapeDtypeStruct(s, d) for s, d in out],
        in_specs=[
            smem if i < scalars else anywhere if i in held else vmem for i in range(len(args))
        ],
        out_specs=[vmem] * len(out),
        scratch_shapes=[pltpu.VMEM(*s) if isinstance(s, tuple) else s for s in scratch],
        compiler_params=PARAMS,
    )(*args)


F32 = jnp.float32
BF16 = jnp.bfloat16
WIDE = ((H + 6, 40, C), F32)


def row_exchange(values, even, pole):
    head, tail = values[:3], values[-3:]
    first, second = row_pairs()
    outer = jnp.where(even, head, tail)
    outer = jnp.where(pole, jnp.flip(outer, 0), outer)
    got_first = lax.ppermute(jnp.where(even, tail, head), AXES, first)
    got_second = lax.ppermute(outer, AXES, second)
    return got_first, got_second


def body(state_field, cotangent, depthwise, norm_gain, w_in, w_out):
    grad_scale = 1.0 / math.sqrt(CELLS * LAT * LON)
    lat, _ = lat_lon()
    lat = lat.astype(jnp.int32)
    even = lat % 2 == 0
    pole = (lat == 0) | (lat == LAT - 1)
    parity = even.astype(jnp.int32)
    core = lax.axis_index("core").astype(jnp.int32).reshape(1)
    cot = cotangent.reshape(CELLS, C)
    gain = norm_gain.reshape(1, C)
    *own_edges, gain, w_in, w_out = call(
        own_edge_kernel,
        [
            ((9 * H, C), F32),
            ((9 * H, C), F32),
            ((1, C), F32),
            ((C, FF), BF16),
            ((FF, C), BF16),
        ],
        state_field, cot, gain, w_in, w_out,
        scratch=[
            ((H, W, C), F32),
            ((CELLS, C), BF16),
            ((CELLS, C), F32),
            pltpu.SemaphoreType.DMA((5,)),
        ],
        held=(0, 1, 2, 3, 4),
    )
    rows = row_exchange(state_field, even, pole)
    above, below, to_right, to_left = call(
        edge_kernel,
        [((3, W, C), F32), ((3, W, C), F32), ((EDGE, C), F32), ((EDGE, C), F32)],
        parity.reshape(1), *rows, *own_edges,
        scalars=1,
    )
    right, left = column_pairs()
    before = lax.ppermute(to_right, AXES, right)
    after = lax.ppermute(to_left, AXES, left)
    pieces = (above, below, state_field, before, after)
    part = ((16, 128, 128), F32)
    mine, theirs, middle, grad_middle, tap_middle = call(
        middle_kernel,
        [part, part, ((HALF_CELLS, FF), BF16), ((H, M, C), F32), ((128, 128), F32)],
        core, above, below, state_field, cot, depthwise, gain, w_in, w_out,
        scratch=[
            ((H + 6, W, C), F32),
            ((HALF_CELLS, C), F32),
            ((H, W, C), F32),
            ((HALF_CELLS, FF), BF16),
        ],
        scalars=1,
    )
    mine, theirs, hidden, grad_pre, centred, inv_std = call(
        forward_kernel,
        [
            part,
            part,
            ((HALF_CELLS, FF), BF16),
            ((HALF_CELLS, FF), BF16),
            ((HALF_CELLS, C), F32),
            ((HALF_CELLS, 128), F32),
        ],
        core, *pieces, cot, depthwise, gain, w_in, w_out, mine, theirs,
        scratch=[WIDE, ((HALF_CELLS, C), F32), ((H, M, C), F32)],
        scalars=1,
    )
    theirs = lax.ppermute(theirs, "core", [(0, 1), (1, 0)])
    grad_conv, taps = call(
        backward_kernel,
        [((H, V, C), F32), ((128, 128), F32)],
        *pieces, gain, w_in, grad_pre, centred, inv_std, grad_middle, tap_middle,
        scratch=[WIDE, ((H, M, C), F32)],
    )
    (joined,) = call(join_kernel, [((16, 136, 128), F32)], mine, theirs, taps)
    plane = lax.all_to_all(joined, ("x", "y"), split_axis=0, concat_axis=0, tiled=True)
    grad_rows = row_exchange(grad_conv, even, pole)
    plane, grad_rows = lax.optimization_barrier((plane, grad_rows))
    (spread,) = call(plane_kernel, [((16, 16, 128), F32)], plane)
    column = lax.all_to_all(spread, ("zh", "zl"), split_axis=0, concat_axis=0, tiled=True)
    grad_input, block_out = call(
        adjoint_kernel,
        [((CELLS, C), BF16), ((CELLS, C), BF16)],
        jnp.stack([lat, parity]), *grad_rows, grad_conv, cot, depthwise, state_field, middle, hidden, w_out,
        scratch=[
            ((H + 6, V, C), F32),
            ((2, 7, 8, C), F32),
            ((CELLS, C), F32),
            ((H, V, C), F32),
        ],
        scalars=1,
    )
    column, grad_input = lax.optimization_barrier((column, grad_input))
    weight_grads, shared = call(
        functools.partial(column_kernel, grad_scale), [((2, 512), F32), ((32, 8, 128), F32)], column
    )
    shared = lax.all_to_all(shared, ("x", "core", "y"), split_axis=0, concat_axis=0, tiled=True)
    tap_total, gain_total = call(total_kernel, [((49, C), F32), ((1, C), F32)], shared)
    return (
        block_out.reshape(H, W, C),
        grad_input.reshape(H, W, C),
        weight_grads,
        tap_total,
        gain_total.reshape(C),
    )


def solution(mesh):
    split = Mesh(mesh.devices.reshape(SIZES), AXES)
    cells = P(("zh", "x", "core"), ("y", "zl"), None)
    return jax.shard_map(
        body,
        mesh=split,
        in_specs=(cells, cells, P(), P(), P(), P()),
        out_specs=(cells, cells, P(AXES, None), P(), P()),
        check_vma=False,
    )
```

```python
import functools
import math

import jax
import jax.numpy as jnp
from jax import lax
from jax.experimental import pallas as pl
from jax.experimental.pallas import tpu as pltpu
from jax.sharding import Mesh, PartitionSpec as P

AXES = ("zh", "x", "core", "y", "zl")
SIZES = (4, 4, 2, 4, 4)
LAT = 32
LON = 16


def lat_lon():
    lat = (lax.axis_index("zh") * 4 + lax.axis_index("x")) * 2 + lax.axis_index("core")
    return lat, lax.axis_index("y") * 4 + lax.axis_index("zl")


def row_pairs():
    first, second = [], []
    for lat in range(LAT):
        for lon in range(LON):
            here = lat * LON + lon
            first.append((here, (lat ^ 1) * LON + lon))
            if lat == 0 or lat == LAT - 1:
                peer = lat * LON + (lon + LON // 2) % LON
            else:
                peer = (lat - 1 if lat % 2 == 0 else lat + 1) * LON + lon
            second.append((here, peer))
    return first, second


def column_pairs():
    right, left = [], []
    for lat in range(LAT):
        for lon in range(LON):
            here = lat * LON + lon
            right.append((here, lat * LON + (lon + 1) % LON))
            left.append((here, lat * LON + (lon - 1) % LON))
    return right, left


H = 12
W = 24
C = 256
FF = 1024
V = 32
CELLS = H * W
M = 16
HALF_CELLS = H * M
OWN = H * 8
EDGE = 6 * (H + 6) + 3 * H
PARAMS = pltpu.CompilerParams(vmem_limit_bytes=20 * 1024 * 1024)


def gelu_parts(values):
    phi = 0.5 * (1.0 + lax.erf(values * 0.7071067811865476))
    slope = phi + values * jnp.exp(-0.5 * values * values) * 0.3989422804014327
    return values * phi, slope


def window(wide_ref, row, col, width, lanes):
    return wide_ref[row, col : col + width, lanes]


def convolve(wide_ref, weight, base, width, lanes):
    total = [None] * H
    for col in range(7):
        for row in range(H + 6):
            part = window(wide_ref, row, base + col, width, lanes)
            for tap in range(7):
                out = row - tap
                if 0 <= out < H:
                    term = weight(row, tap, col, lanes) * part
                    total[out] = term if total[out] is None else total[out] + term
    return total


def own_edge_kernel(
    state_hbm, cot_hbm, gain_hbm, w_in_hbm, w_out_hbm,
    to_right, to_left, gain, w_in, w_out,
    state, cot, full, sem,
):
    fetches = [
        pltpu.make_async_copy(source, target, sem.at[i])
        for i, (source, target) in enumerate(
            (
                (state_hbm, state),
                (cot_hbm, cot),
                (gain_hbm, gain),
                (w_in_hbm, w_in),
                (w_out_hbm, w_out),
            )
        )
    ]
    for fetch in fetches:
        fetch.start()
    fetches[0].wait()
    for row in range(H):
        to_right[6 * row : 6 * row + 6, :] = state[row, W - 6 : W, :]
        to_left[6 * row : 6 * row + 6, :] = state[row, 0:6, :]
    fetches[1].wait()
    full[...] = cot[...].astype(jnp.float32)
    for row in range(H):
        place = 6 * H + 3 * row
        to_right[place : place + 3, :] = full[W * row + W - 3 : W * row + W, :]
        to_left[place : place + 3, :] = full[W * row : W * row + 3, :]
    for fetch in fetches[2:]:
        fetch.wait()


def edge_kernel(even_ref, first, second, own_right, own_left, above, below, to_right, to_left):
    even = even_ref[0] == 1
    above[...] = jnp.where(even, second[...], first[...])
    below[...] = jnp.where(even, first[...], second[...])
    to_right[0 : 9 * H, :] = own_right[...]
    to_left[0 : 9 * H, :] = own_left[...]
    for row in range(3):
        for place, ref in ((9 * H, above), (9 * H + 18, below)):
            spot = place + 6 * row
            to_right[spot : spot + 6, :] = ref[row, W - 6 : W, :]
            to_left[spot : spot + 6, :] = ref[row, 0:6, :]


def source_row(above, state, below, row):
    if row < 3:
        return above[row], 9 * H + 6 * row
    if row < H + 3:
        return state[row - 3], 6 * (row - 3)
    return below[row - H - 3], 9 * H + 18 + 6 * (row - H - 3)


def normalise(values):
    centred = values - jnp.mean(values, axis=-1, keepdims=True)
    variance = jnp.mean(centred * centred, axis=-1, keepdims=True)
    inv_std = 1.0 / jnp.sqrt(variance + 1e-06)
    return centred * inv_std, inv_std


def activate(normed, cotangent, w_in, w_out, hidden, grad_pre):
    for part in range(4):
        cols = slice(256 * part, 256 * part + 256)
        pre_act = jnp.dot(normed, w_in[:, cols], preferred_element_type=jnp.float32)
        grad_hidden = lax.dot_general(
            cotangent, w_out[cols, :], (((1,), (1,)), ((), ())), preferred_element_type=jnp.float32
        )
        value, slope = gelu_parts(pre_act)
        hidden[:, cols] = value.astype(jnp.bfloat16)
        grad_pre[:, cols] = (grad_hidden * slope).astype(jnp.bfloat16)


def weight_products(core, grad_pre, normed, hidden, cotangent, mine, theirs, before):
    for part in range(4):
        cols = slice(256 * part, 256 * part + 256)
        for side, (left, right) in enumerate(((grad_pre[:, cols], normed), (hidden[:, cols], cotangent))):
            product = lax.dot_general(
                left, right, (((0,), (0,)), ((), ())), preferred_element_type=jnp.float32
            )
            for x in range(4):
                for run in range(2):
                    lanes = slice(128 * run, 128 * run + 128)
                    ours = product[64 * x : 64 * x + 32, lanes]
                    other = product[64 * x + 32 : 64 * x + 64, lanes]
                    keep = jnp.where(core == 0, ours, other).reshape(4, 8, 128)
                    send = jnp.where(core == 0, other, ours).reshape(4, 8, 128)
                    row = 32 * (2 * side + run) + 8 * part
                    places = (slice(4 * x, 4 * x + 4), slice(row, row + 8), slice(None))
                    if before is not None:
                        keep = keep + before[0][places]
                        send = send + before[1][places]
                    mine[places] = keep
                    theirs[places] = send


def norm_gradient(grad_pre, w_in, gain, centred, inv_std):
    grad_normed = lax.dot_general(
        grad_pre, w_in, (((1,), (1,)), ((), ())), preferred_element_type=jnp.float32
    )
    scaled = grad_normed * gain
    grad = inv_std * (
        scaled
        - jnp.mean(scaled, axis=-1, keepdims=True)
        - centred * jnp.mean(scaled * centred, axis=-1, keepdims=True)
    )
    return grad, grad_normed * centred


def tap_sums(wide, starts, grads, out, gain_sum, before):
    for half in range(2):
        lanes = slice(128 * half, 128 * half + 128)
        pieces = grads(lanes)
        for col in range(7):
            total = [jnp.zeros((8, 128), jnp.float32)] * 7
            for row in range(H + 6):
                for start, piece in zip(starts, pieces):
                    width = piece[0].shape[0]
                    part = window(wide, row, start + col, width, lanes)
                    for tap in range(7):
                        if 0 <= row - tap < H:
                            term = part * piece[row - tap]
                            for tile in range(0, width, 8):
                                total[tap] = total[tap] + term[tile : tile + 8]
            for tap in range(7):
                spot = 64 * half + 7 * tap + col
                value = jnp.sum(total[tap], axis=0, keepdims=True)
                out[spot : spot + 1, :] = (
                    value if before is None else value + before[spot : spot + 1, :]
                )
        spot = 64 * half + 49
        value = gain_sum[:, lanes]
        out[spot : spot + 1, :] = value if before is None else value + before[spot : spot + 1, :]
        out[spot + 1 : spot + 15, :] = jnp.zeros((14, 128), jnp.float32)


def tap_weight(taps):
    return lambda row, tap, col, lanes: taps[7 * tap + col : 7 * tap + col + 1, lanes]


def middle_kernel(
    core_ref, above, below, state, cot, taps, gain, w_in, w_out,
    mine, theirs, hidden, grad_out, tap_out,
    wide, conv, full, grad_pre,
):
    wide[0:3] = above[...]
    wide[3 : 3 + H] = state[...]
    wide[3 + H :] = below[...]
    full[...] = cot[...].astype(jnp.float32).reshape(H, W, C)
    for half in range(2):
        lanes = slice(128 * half, 128 * half + 128)
        total = convolve(wide, tap_weight(taps), 2, M, lanes)
        for out in range(H):
            conv[M * out : M * out + M, lanes] = total[out]
    centred, inv_std = normalise(conv[...])
    normed = (centred * gain[...]).astype(jnp.bfloat16)
    cotangent = full[:, 5 : 5 + M, :].reshape(HALF_CELLS, C).astype(jnp.bfloat16)
    activate(normed, cotangent, w_in, w_out, hidden, grad_pre)
    weight_products(core_ref[0], grad_pre, normed, hidden, cotangent, mine, theirs, None)
    grad, gains = norm_gradient(grad_pre[...], w_in[...], gain[...], centred, inv_std)
    grad_out[...] = grad.reshape(H, M, C)
    tap_sums(
        wide,
        (2,),
        lambda lanes: [[grad_out[row, :, lanes] for row in range(H)]],
        tap_out,
        jnp.sum(gains, axis=0, keepdims=True),
        None,
    )


def fill(wide, above, below, state, before, after):
    wide[:, 32:40, :] = jnp.zeros((H + 6, 8, C), jnp.float32)
    for row in range(H + 6):
        centre, spot = source_row(above, state, below, row)
        wide[row, 8 : 8 + W, :] = centre
        wide[row, 2:8, :] = before[spot : spot + 6, :]
        wide[row, 8 + W : 14 + W, :] = after[spot : spot + 6, :]


def forward_kernel(
    core_ref, above, below, state, before, after, cot, taps, gain, w_in, w_out, mine_in, theirs_in,
    mine, theirs, hidden, grad_pre, centred_out, inv_out,
    wide, conv, cot_all,
):
    fill(wide, above, below, state, before, after)
    cot_all[H:, :, :] = jnp.zeros((H, 8, C), jnp.float32)
    own = cot[...].astype(jnp.float32)
    for row in range(H):
        place = 6 * H + 3 * row
        cot_all[row, 0:5, :] = own[W * row : W * row + 5]
        cot_all[row, 5:8, :] = own[W * row + W - 3 : W * row + W]
        cot_all[H + row, 0:3, :] = before[place : place + 3, :]
        cot_all[H + row, 3:6, :] = after[place : place + 3, :]
    for half in range(2):
        lanes = slice(128 * half, 128 * half + 128)
        west = convolve(wide, tap_weight(taps), 2, 8, lanes)
        east = convolve(wide, tap_weight(taps), 26, 8, lanes)
        for out in range(H):
            spot = 8 * out
            conv[spot : spot + 5, lanes] = west[out][3:8]
            conv[spot + 5 : spot + 8, lanes] = east[out][0:3]
            spot = OWN + 8 * out
            conv[spot : spot + 3, lanes] = west[out][0:3]
            conv[spot + 3 : spot + 8, lanes] = east[out][3:8]
    centred, inv_std = normalise(conv[...])
    centred_out[...] = centred
    inv_out[...] = jnp.broadcast_to(inv_std, (HALF_CELLS, 128))
    normed = (centred * gain[...]).astype(jnp.bfloat16)
    cotangent = cot_all[...].reshape(HALF_CELLS, C).astype(jnp.bfloat16)
    activate(normed, cotangent, w_in, w_out, hidden, grad_pre)
    own_rows = slice(0, OWN)
    weight_products(
        core_ref[0],
        grad_pre[own_rows, :],
        normed[own_rows],
        hidden[own_rows, :],
        cotangent[own_rows],
        mine,
        theirs,
        (mine_in, theirs_in),
    )


def backward_kernel(
    above, below, state, before, after, gain, w_in, grad_pre, centred_in, inv_in, grad_mid, tap_mid,
    grad_conv, out,
    wide, own_grad,
):
    fill(wide, above, below, state, before, after)
    grad, gains = norm_gradient(grad_pre[...], w_in[...], gain[...], centred_in[...], inv_in[...][:, 0:1])
    own = grad[0:OWN].reshape(H, 8, C)
    rest = grad[OWN:].reshape(H, 8, C)
    own_grad[...] = jnp.zeros((H, M, C), jnp.float32)
    own_grad[:, 3:8, :] = own[:, 0:5]
    own_grad[:, 8:11, :] = own[:, 5:8]
    grad_conv[:, 0:3, :] = rest[:, 0:3]
    grad_conv[:, 3:8, :] = own[:, 0:5]
    grad_conv[:, 24:27, :] = own[:, 5:8]
    grad_conv[:, 27:32, :] = rest[:, 3:8]
    grad_conv[:, 8:24, :] = grad_mid[...]
    tap_sums(
        wide,
        (2, 26),
        lambda lanes: [
            [own_grad[row, spot : spot + 8, lanes] for row in range(H)] for spot in (0, 8)
        ],
        out,
        jnp.sum(gains[0:OWN], axis=0, keepdims=True),
        tap_mid,
    )


def adjoint_kernel(
    where_ref, first, second, grad_conv, cot, taps, state, middle, outer, w_out,
    out, block_out,
    wide, rim, grad, branch_ref,
):
    branch = jnp.dot(middle[...], w_out[...], preferred_element_type=jnp.float32)
    branch_ref[:, 8:24, :] = branch.reshape(H, M, C)
    branch = jnp.dot(outer[0:OWN, :], w_out[...], preferred_element_type=jnp.float32)
    branch = branch.reshape(H, 8, C)
    branch_ref[:, 3:8, :] = branch[:, 0:5]
    branch_ref[:, 24:27, :] = branch[:, 5:8]
    block_out[...] = (state[...] + branch_ref[:, 3 : 3 + W, :]).reshape(CELLS, C).astype(jnp.bfloat16)
    lat = where_ref[0]
    even = where_ref[1] == 1
    wide[0:3] = jnp.where(even, second[...], first[...])
    wide[3 : 3 + H] = grad_conv[...]
    wide[3 + H :] = jnp.where(even, first[...], second[...])
    for tap in range(7):
        here = taps[7 * tap : 7 * tap + 7, :]
        turned = taps[7 * (6 - tap) : 7 * (6 - tap) + 7, :]
        rim[0, tap, 0:7, :] = jnp.where(lat == 0, turned, here)
        rim[1, tap, 0:7, :] = jnp.where(lat == LAT - 1, turned, here)

    def weight(row, tap, col, lanes):
        if row < 3:
            return rim[0, 6 - tap, 6 - col : 7 - col, lanes]
        if row >= H + 3:
            return rim[1, 6 - tap, 6 - col : 7 - col, lanes]
        place = 7 * (6 - tap) + 6 - col
        return taps[place : place + 1, lanes]

    for half in range(2):
        lanes = slice(128 * half, 128 * half + 128)
        total = convolve(wide, weight, 0, W, lanes)
        for row in range(H):
            grad[W * row : W * row + W, lanes] = total[row]
    out[...] = (cot[...].astype(jnp.float32) + grad[...]).astype(jnp.bfloat16)


def join_kernel(mine, theirs, taps, out):
    out[:, 0:128, :] = mine[...] + theirs[...]
    out[:, 128:136, :] = taps[...].reshape(16, 8, 128)


def plane_kernel(got, out):
    total = got[0]
    for peer in range(1, 16):
        total = total + got[peer]
    for zh in range(4):
        for zl in range(4):
            place = 4 * zh + zl
            for run in range(4):
                row = 32 * run + 8 * zh + 2 * zl
                out[place, 2 * run : 2 * run + 2, :] = total[row : row + 2]
            out[place, 8:16, :] = total[128:136]


def share_kernel(scale, got, shared):
    total = got[0, 8:16, :]
    for peer in range(1, 16):
        total = total + got[peer, 8:16, :]
    total = total * scale
    for peer in range(32):
        shared[peer] = total


def column_kernel(scale, got, weight_grads):
    total = got[0, 0:8, :]
    for peer in range(1, 16):
        total = total + got[peer, 0:8, :]
    total = total * scale
    for run in range(4):
        weight_grads[:, 128 * run : 128 * run + 128] = total[2 * run : 2 * run + 2]


def total_kernel(got, taps, gain):
    for half in range(2):
        rows = []
        for place in range(8 * half, 8 * half + 8):
            x, y = place // 4, place % 4
            rows.append(got[8 * x + y] + got[8 * x + 4 + y])
        table = jnp.concatenate(rows, 0)
        taps[:, 128 * half : 128 * half + 128] = table[0:49]
        gain[:, 128 * half : 128 * half + 128] = table[49:50]


def call(kernel, out, *args, scratch=(), scalars=0, held=()):
    vmem = pl.BlockSpec(memory_space=pltpu.VMEM)
    smem = pl.BlockSpec(memory_space=pltpu.SMEM)
    anywhere = pl.BlockSpec(memory_space=pltpu.HBM)
    return pl.pallas_call(
        kernel,
        out_shape=[jax.ShapeDtypeStruct(s, d) for s, d in out],
        in_specs=[
            smem if i < scalars else anywhere if i in held else vmem for i in range(len(args))
        ],
        out_specs=[vmem] * len(out),
        scratch_shapes=[pltpu.VMEM(*s) if isinstance(s, tuple) else s for s in scratch],
        compiler_params=PARAMS,
    )(*args)


F32 = jnp.float32
BF16 = jnp.bfloat16
WIDE = ((H + 6, 40, C), F32)


def row_exchange(values, even, pole):
    head, tail = values[:3], values[-3:]
    first, second = row_pairs()
    outer = jnp.where(even, head, tail)
    outer = jnp.where(pole, jnp.flip(outer, 0), outer)
    got_first = lax.ppermute(jnp.where(even, tail, head), AXES, first)
    got_second = lax.ppermute(outer, AXES, second)
    return got_first, got_second


def body(state_field, cotangent, depthwise, norm_gain, w_in, w_out):
    grad_scale = 1.0 / math.sqrt(CELLS * LAT * LON)
    lat, _ = lat_lon()
    lat = lat.astype(jnp.int32)
    even = lat % 2 == 0
    pole = (lat == 0) | (lat == LAT - 1)
    parity = even.astype(jnp.int32)
    core = lax.axis_index("core").astype(jnp.int32).reshape(1)
    cot = cotangent.reshape(CELLS, C)
    gain = norm_gain.reshape(1, C)
    *own_edges, gain, w_in, w_out = call(
        own_edge_kernel,
        [
            ((9 * H, C), F32),
            ((9 * H, C), F32),
            ((1, C), F32),
            ((C, FF), BF16),
            ((FF, C), BF16),
        ],
        state_field, cot, gain, w_in, w_out,
        scratch=[
            ((H, W, C), F32),
            ((CELLS, C), BF16),
            ((CELLS, C), F32),
            pltpu.SemaphoreType.DMA((5,)),
        ],
        held=(0, 1, 2, 3, 4),
    )
    rows = row_exchange(state_field, even, pole)
    above, below, to_right, to_left = call(
        edge_kernel,
        [((3, W, C), F32), ((3, W, C), F32), ((EDGE, C), F32), ((EDGE, C), F32)],
        parity.reshape(1), *rows, *own_edges,
        scalars=1,
    )
    right, left = column_pairs()
    before = lax.ppermute(to_right, AXES, right)
    after = lax.ppermute(to_left, AXES, left)
    pieces = (above, below, state_field, before, after)
    part = ((16, 128, 128), F32)
    mine, theirs, middle, grad_middle, tap_middle = call(
        middle_kernel,
        [part, part, ((HALF_CELLS, FF), BF16), ((H, M, C), F32), ((128, 128), F32)],
        core, above, below, state_field, cot, depthwise, gain, w_in, w_out,
        scratch=[
            ((H + 6, W, C), F32),
            ((HALF_CELLS, C), F32),
            ((H, W, C), F32),
            ((HALF_CELLS, FF), BF16),
        ],
        scalars=1,
    )
    mine, theirs, hidden, grad_pre, centred, inv_std = call(
        forward_kernel,
        [
            part,
            part,
            ((HALF_CELLS, FF), BF16),
            ((HALF_CELLS, FF), BF16),
            ((HALF_CELLS, C), F32),
            ((HALF_CELLS, 128), F32),
        ],
        core, *pieces, cot, depthwise, gain, w_in, w_out, mine, theirs,
        scratch=[WIDE, ((HALF_CELLS, C), F32), ((2 * H, 8, C), F32)],
        scalars=1,
    )
    theirs = lax.ppermute(theirs, "core", [(0, 1), (1, 0)])
    grad_conv, taps = call(
        backward_kernel,
        [((H, V, C), F32), ((128, 128), F32)],
        *pieces, gain, w_in, grad_pre, centred, inv_std, grad_middle, tap_middle,
        scratch=[WIDE, ((H, M, C), F32)],
    )
    (joined,) = call(join_kernel, [((16, 136, 128), F32)], mine, theirs, taps)
    plane = lax.all_to_all(joined, ("x", "y"), split_axis=0, concat_axis=0, tiled=True)
    grad_rows = row_exchange(grad_conv, even, pole)
    plane, grad_rows = lax.optimization_barrier((plane, grad_rows))
    (spread,) = call(plane_kernel, [((16, 16, 128), F32)], plane)
    column = lax.all_to_all(spread, ("zh", "zl"), split_axis=0, concat_axis=0, tiled=True)
    grad_input, block_out = call(
        adjoint_kernel,
        [((CELLS, C), BF16), ((CELLS, C), BF16)],
        jnp.stack([lat, parity]), *grad_rows, grad_conv, cot, depthwise, state_field, middle, hidden, w_out,
        scratch=[
            ((H + 6, V, C), F32),
            ((2, 7, 8, C), F32),
            ((CELLS, C), F32),
            ((H, V, C), F32),
        ],
        scalars=1,
    )
    column, grad_input = lax.optimization_barrier((column, grad_input))
    (shared,) = call(functools.partial(share_kernel, grad_scale), [((32, 8, 128), F32)], column)
    (weight_grads,) = call(functools.partial(column_kernel, grad_scale), [((2, 512), F32)], column)
    shared = lax.all_to_all(shared, ("x", "core", "y"), split_axis=0, concat_axis=0, tiled=True)
    tap_total, gain_total = call(total_kernel, [((49, C), F32), ((1, C), F32)], shared)
    return (
        block_out.reshape(H, W, C),
        grad_input.reshape(H, W, C),
        weight_grads,
        tap_total,
        gain_total.reshape(C),
    )


def solution(mesh):
    split = Mesh(mesh.devices.reshape(SIZES), AXES)
    cells = P(("zh", "x", "core"), ("y", "zl"), None)
    return jax.shard_map(
        body,
        mesh=split,
        in_specs=(cells, cells, P(), P(), P(), P()),
        out_specs=(cells, cells, P(AXES, None), P(), P()),
        check_vma=False,
    )
```

```python
import functools
import math

import jax
import jax.numpy as jnp
from jax import lax
from jax.experimental import pallas as pl
from jax.experimental.pallas import tpu as pltpu
from jax.sharding import Mesh, PartitionSpec as P

AXES = ("zh", "x", "core", "y", "zl")
SIZES = (4, 4, 2, 4, 4)
LAT = 32
LON = 16


def lat_lon():
    lat = (lax.axis_index("zh") * 4 + lax.axis_index("x")) * 2 + lax.axis_index("core")
    return lat, lax.axis_index("y") * 4 + lax.axis_index("zl")


def row_pairs():
    first, second = [], []
    for lat in range(LAT):
        for lon in range(LON):
            here = lat * LON + lon
            first.append((here, (lat ^ 1) * LON + lon))
            if lat == 0 or lat == LAT - 1:
                peer = lat * LON + (lon + LON // 2) % LON
            else:
                peer = (lat - 1 if lat % 2 == 0 else lat + 1) * LON + lon
            second.append((here, peer))
    return first, second


def column_pairs():
    near, far = [], []
    for lat in range(LAT):
        for lon in range(LON):
            here = lat * LON + lon
            near.append((here, lat * LON + (lon ^ 1)))
            far.append((here, lat * LON + (lon - 1 if lon % 2 == 0 else lon + 1) % LON))
    return near, far


H = 12
W = 24
C = 256
FF = 1024
V = 32
CELLS = H * W
M = 16
HALF_CELLS = H * M
EDGE = 6 * (H + 6) + 3 * H
PARAMS = pltpu.CompilerParams(vmem_limit_bytes=20 * 1024 * 1024)


def gelu_parts(values):
    phi = 0.5 * (1.0 + lax.erf(values * 0.7071067811865476))
    slope = phi + values * jnp.exp(-0.5 * values * values) * 0.3989422804014327
    return values * phi, slope


def window(wide_ref, row, col, width, lanes):
    return wide_ref[row, col : col + width, lanes]


def convolve(wide_ref, weight, base, width, lanes):
    total = [None] * H
    for col in range(7):
        for row in range(H + 6):
            part = window(wide_ref, row, base + col, width, lanes)
            for tap in range(7):
                out = row - tap
                if 0 <= out < H:
                    term = weight(row, tap, col, lanes) * part
                    total[out] = term if total[out] is None else total[out] + term
    return total


def own_edge_kernel(
    state_hbm, cot_hbm, gain_hbm, w_in_hbm, w_out_hbm,
    to_right, to_left, gain, w_in, w_out,
    state, cot, full, sem,
):
    fetches = [
        pltpu.make_async_copy(source, target, sem.at[i])
        for i, (source, target) in enumerate(
            (
                (state_hbm, state),
                (cot_hbm, cot),
                (gain_hbm, gain),
                (w_in_hbm, w_in),
                (w_out_hbm, w_out),
            )
        )
    ]
    for fetch in fetches:
        fetch.start()
    fetches[0].wait()
    for row in range(H):
        to_right[6 * row : 6 * row + 6, :] = state[row, W - 6 : W, :]
        to_left[6 * row : 6 * row + 6, :] = state[row, 0:6, :]
    fetches[1].wait()
    full[...] = cot[...].astype(jnp.float32)
    for row in range(H):
        place = 6 * H + 3 * row
        to_right[place : place + 3, :] = full[W * row + W - 3 : W * row + W, :]
        to_left[place : place + 3, :] = full[W * row : W * row + 3, :]
    for fetch in fetches[2:]:
        fetch.wait()


def edge_kernel(even_ref, first, second, own_right, own_left, above, below, near, far):
    even = even_ref[0] == 1
    west = even_ref[1] == 1
    above[...] = jnp.where(even, second[...], first[...])
    below[...] = jnp.where(even, first[...], second[...])
    far[0 : 9 * H, :] = jnp.where(west, own_left[...], own_right[...])
    near[0 : 9 * H, :] = jnp.where(west, own_right[...], own_left[...])
    for row in range(3):
        for place, ref in ((9 * H, above), (9 * H + 18, below)):
            spot = place + 6 * row
            to_right = ref[row, W - 6 : W, :]
            to_left = ref[row, 0:6, :]
            far[spot : spot + 6, :] = jnp.where(west, to_left, to_right)
            near[spot : spot + 6, :] = jnp.where(west, to_right, to_left)


def source_row(above, state, below, row):
    if row < 3:
        return above[row], 9 * H + 6 * row
    if row < H + 3:
        return state[row - 3], 6 * (row - 3)
    return below[row - H - 3], 9 * H + 18 + 6 * (row - H - 3)


def normalise(values):
    centred = values - jnp.mean(values, axis=-1, keepdims=True)
    variance = jnp.mean(centred * centred, axis=-1, keepdims=True)
    inv_std = 1.0 / jnp.sqrt(variance + 1e-06)
    return centred * inv_std, inv_std


def activate(normed, cotangent, w_in, w_out, hidden, grad_pre):
    for part in range(4):
        cols = slice(256 * part, 256 * part + 256)
        pre_act = jnp.dot(normed, w_in[:, cols], preferred_element_type=jnp.float32)
        grad_hidden = lax.dot_general(
            cotangent, w_out[cols, :], (((1,), (1,)), ((), ())), preferred_element_type=jnp.float32
        )
        value, slope = gelu_parts(pre_act)
        hidden[:, cols] = value.astype(jnp.bfloat16)
        grad_pre[:, cols] = (grad_hidden * slope).astype(jnp.bfloat16)


def weight_products(core, grad_pre, normed, hidden, cotangent, mine, theirs, before):
    for part in range(4):
        cols = slice(256 * part, 256 * part + 256)
        for side, (left, right) in enumerate(((grad_pre[:, cols], normed), (hidden[:, cols], cotangent))):
            product = lax.dot_general(
                left, right, (((0,), (0,)), ((), ())), preferred_element_type=jnp.float32
            )
            for x in range(4):
                for run in range(2):
                    lanes = slice(128 * run, 128 * run + 128)
                    ours = product[64 * x : 64 * x + 32, lanes]
                    other = product[64 * x + 32 : 64 * x + 64, lanes]
                    keep = jnp.where(core == 0, ours, other).reshape(4, 8, 128)
                    send = jnp.where(core == 0, other, ours).reshape(4, 8, 128)
                    row = 32 * (2 * side + run) + 8 * part
                    places = (slice(4 * x, 4 * x + 4), slice(row, row + 8), slice(None))
                    if before is not None:
                        keep = keep + before[0][places]
                        send = send + before[1][places]
                    mine[places] = keep
                    theirs[places] = send


def norm_gradient(grad_pre, w_in, gain, centred, inv_std):
    grad_normed = lax.dot_general(
        grad_pre, w_in, (((1,), (1,)), ((), ())), preferred_element_type=jnp.float32
    )
    scaled = grad_normed * gain
    grad = inv_std * (
        scaled
        - jnp.mean(scaled, axis=-1, keepdims=True)
        - centred * jnp.mean(scaled * centred, axis=-1, keepdims=True)
    )
    return grad, grad_normed * centred


def tap_sums(wide, starts, grads, out, gain_sum, before):
    for half in range(2):
        lanes = slice(128 * half, 128 * half + 128)
        pieces = grads(lanes)
        for col in range(7):
            total = [jnp.zeros((8, 128), jnp.float32)] * 7
            for row in range(H + 6):
                for start, piece in zip(starts, pieces):
                    width = piece[0].shape[0]
                    part = window(wide, row, start + col, width, lanes)
                    for tap in range(7):
                        if 0 <= row - tap < H:
                            term = part * piece[row - tap]
                            for tile in range(0, width, 8):
                                total[tap] = total[tap] + term[tile : tile + 8]
            for tap in range(7):
                spot = 64 * half + 7 * tap + col
                value = jnp.sum(total[tap], axis=0, keepdims=True)
                out[spot : spot + 1, :] = (
                    value if before is None else value + before[spot : spot + 1, :]
                )
        spot = 64 * half + 49
        value = gain_sum[:, lanes]
        out[spot : spot + 1, :] = value if before is None else value + before[spot : spot + 1, :]
        out[spot + 1 : spot + 15, :] = jnp.zeros((14, 128), jnp.float32)


def tap_weight(taps):
    return lambda row, tap, col, lanes: taps[7 * tap + col : 7 * tap + col + 1, lanes]


def middle_kernel(
    core_ref, above, below, state, cot, taps, gain, w_in, w_out,
    mine, theirs, hidden, grad_out, tap_out,
    wide, conv, full, grad_pre,
):
    wide[0:3] = above[...]
    wide[3 : 3 + H] = state[...]
    wide[3 + H :] = below[...]
    full[...] = cot[...].astype(jnp.float32).reshape(H, W, C)
    for half in range(2):
        lanes = slice(128 * half, 128 * half + 128)
        total = convolve(wide, tap_weight(taps), 2, M, lanes)
        for out in range(H):
            conv[M * out : M * out + M, lanes] = total[out]
    centred, inv_std = normalise(conv[...])
    normed = (centred * gain[...]).astype(jnp.bfloat16)
    cotangent = full[:, 5 : 5 + M, :].reshape(HALF_CELLS, C).astype(jnp.bfloat16)
    activate(normed, cotangent, w_in, w_out, hidden, grad_pre)
    weight_products(core_ref[0], grad_pre, normed, hidden, cotangent, mine, theirs, None)
    grad, gains = norm_gradient(grad_pre[...], w_in[...], gain[...], centred, inv_std)
    grad_out[...] = grad.reshape(H, M, C)
    tap_sums(
        wide,
        (2,),
        lambda lanes: [[grad_out[row, :, lanes] for row in range(H)]],
        tap_out,
        jnp.sum(gains, axis=0, keepdims=True),
        None,
    )


def fill(wide, above, below, state, before, after):
    wide[:, 32:40, :] = jnp.zeros((H + 6, 8, C), jnp.float32)
    for row in range(H + 6):
        centre, spot = source_row(above, state, below, row)
        wide[row, 8 : 8 + W, :] = centre
        wide[row, 2:8, :] = before[spot : spot + 6, :]
        wide[row, 8 + W : 14 + W, :] = after[spot : spot + 6, :]


def forward_kernel(
    core_ref, above, below, state, near, far, cot, taps, gain, w_in, w_out, mine_in, theirs_in,
    mine, theirs, hidden, grad_pre, centred_out, inv_out, before, after,
    wide, conv, cot_all,
):
    west = core_ref[1] == 1
    before[...] = jnp.where(west, far[...], near[...])
    after[...] = jnp.where(west, near[...], far[...])
    fill(wide, above, below, state, before, after)
    cot_all[:, 8:16, :] = jnp.zeros((H, 8, C), jnp.float32)
    own = cot[...].astype(jnp.float32)
    for row in range(H):
        place = 6 * H + 3 * row
        cot_all[row, 0:3, :] = before[place : place + 3, :]
        cot_all[row, 3:8, :] = own[W * row : W * row + 5]
        cot_all[row, 8:11, :] = own[W * row + W - 3 : W * row + W]
        cot_all[row, 11:14, :] = after[place : place + 3, :]
    for half in range(2):
        lanes = slice(128 * half, 128 * half + 128)
        for side, base in enumerate((2, 26)):
            total = convolve(wide, tap_weight(taps), base, 8, lanes)
            for out in range(H):
                spot = M * out + 8 * side
                conv[spot : spot + 8, lanes] = total[out]
    centred, inv_std = normalise(conv[...])
    centred_out[...] = centred
    inv_out[...] = jnp.broadcast_to(inv_std, (HALF_CELLS, 128))
    inside = is_inside()
    normed = centred * gain[...]
    own_normed = jnp.where(inside, normed, 0.0).astype(jnp.bfloat16)
    normed = normed.astype(jnp.bfloat16)
    cotangent = cot_all[...].reshape(HALF_CELLS, C)
    own_cot = jnp.where(inside, cotangent, 0.0).astype(jnp.bfloat16)
    cotangent = cotangent.astype(jnp.bfloat16)
    activate(normed, cotangent, w_in, w_out, hidden, grad_pre)
    weight_products(
        core_ref[0], grad_pre, own_normed, hidden, own_cot, mine, theirs, (mine_in, theirs_in)
    )


def is_inside():
    place = lax.broadcasted_iota(jnp.int32, (H, M, C), 1).reshape(HALF_CELLS, C)
    return (place >= 3) & (place < 11)


def backward_kernel(
    above, below, state, before, after, gain, w_in, grad_pre, centred_in, inv_in, grad_mid, tap_mid,
    grad_conv, out,
    wide, own_grad,
):
    fill(wide, above, below, state, before, after)
    grad, gains = norm_gradient(grad_pre[...], w_in[...], gain[...], centred_in[...], inv_in[...][:, 0:1])
    inside = is_inside()
    own_grad[...] = jnp.where(inside, grad, 0.0).reshape(H, M, C)
    grad = grad.reshape(H, M, C)
    grad_conv[:, 0:8, :] = grad[:, 0:8]
    grad_conv[:, 8:24, :] = grad_mid[...]
    grad_conv[:, 24:32, :] = grad[:, 8:16]
    tap_sums(
        wide,
        (2, 26),
        lambda lanes: [
            [own_grad[row, spot : spot + 8, lanes] for row in range(H)] for spot in (0, 8)
        ],
        out,
        jnp.sum(jnp.where(inside, gains, 0.0), axis=0, keepdims=True),
        tap_mid,
    )


def adjoint_kernel(
    where_ref, first, second, grad_conv, cot, taps, state, middle, outer, w_out,
    out, block_out,
    wide, rim, grad, branch_ref,
):
    branch = jnp.dot(middle[...], w_out[...], preferred_element_type=jnp.float32)
    branch_ref[:, 8:24, :] = branch.reshape(H, M, C)
    branch = jnp.dot(outer[...], w_out[...], preferred_element_type=jnp.float32).reshape(H, M, C)
    branch_ref[:, 0:8, :] = branch[:, 0:8]
    branch_ref[:, 24:32, :] = branch[:, 8:16]
    block_out[...] = (state[...] + branch_ref[:, 3 : 3 + W, :]).reshape(CELLS, C).astype(jnp.bfloat16)
    lat = where_ref[0]
    even = where_ref[1] == 1
    wide[0:3] = jnp.where(even, second[...], first[...])
    wide[3 : 3 + H] = grad_conv[...]
    wide[3 + H :] = jnp.where(even, first[...], second[...])
    for tap in range(7):
        here = taps[7 * tap : 7 * tap + 7, :]
        turned = taps[7 * (6 - tap) : 7 * (6 - tap) + 7, :]
        rim[0, tap, 0:7, :] = jnp.where(lat == 0, turned, here)
        rim[1, tap, 0:7, :] = jnp.where(lat == LAT - 1, turned, here)

    def weight(row, tap, col, lanes):
        if row < 3:
            return rim[0, 6 - tap, 6 - col : 7 - col, lanes]
        if row >= H + 3:
            return rim[1, 6 - tap, 6 - col : 7 - col, lanes]
        place = 7 * (6 - tap) + 6 - col
        return taps[place : place + 1, lanes]

    for half in range(2):
        lanes = slice(128 * half, 128 * half + 128)
        total = convolve(wide, weight, 0, W, lanes)
        for row in range(H):
            grad[W * row : W * row + W, lanes] = total[row]
    out[...] = (cot[...].astype(jnp.float32) + grad[...]).astype(jnp.bfloat16)


def join_kernel(mine, theirs, taps, out):
    out[:, 0:128, :] = mine[...] + theirs[...]
    out[:, 128:136, :] = taps[...].reshape(16, 8, 128)


def plane_kernel(got, out):
    total = got[0]
    for peer in range(1, 16):
        total = total + got[peer]
    for zh in range(4):
        for zl in range(4):
            place = 4 * zh + zl
            for run in range(4):
                row = 32 * run + 8 * zh + 2 * zl
                out[place, 2 * run : 2 * run + 2, :] = total[row : row + 2]
            out[place, 8:16, :] = total[128:136]


def column_kernel(scale, got, weight_grads, shared):
    total = got[0]
    for peer in range(1, 16):
        total = total + got[peer]
    total = total * scale
    for run in range(4):
        weight_grads[:, 128 * run : 128 * run + 128] = total[2 * run : 2 * run + 2]
    for peer in range(32):
        shared[peer] = total[8:16]


def total_kernel(got, taps, gain):
    for half in range(2):
        rows = []
        for place in range(8 * half, 8 * half + 8):
            x, y = place // 4, place % 4
            rows.append(got[8 * x + y] + got[8 * x + 4 + y])
        table = jnp.concatenate(rows, 0)
        taps[:, 128 * half : 128 * half + 128] = table[0:49]
        gain[:, 128 * half : 128 * half + 128] = table[49:50]


def call(kernel, out, *args, scratch=(), scalars=0, held=()):
    vmem = pl.BlockSpec(memory_space=pltpu.VMEM)
    smem = pl.BlockSpec(memory_space=pltpu.SMEM)
    anywhere = pl.BlockSpec(memory_space=pltpu.HBM)
    return pl.pallas_call(
        kernel,
        out_shape=[jax.ShapeDtypeStruct(s, d) for s, d in out],
        in_specs=[
            smem if i < scalars else anywhere if i in held else vmem for i in range(len(args))
        ],
        out_specs=[vmem] * len(out),
        scratch_shapes=[pltpu.VMEM(*s) if isinstance(s, tuple) else s for s in scratch],
        compiler_params=PARAMS,
    )(*args)


F32 = jnp.float32
BF16 = jnp.bfloat16
WIDE = ((H + 6, 40, C), F32)


def row_exchange(values, even, pole):
    head, tail = values[:3], values[-3:]
    first, second = row_pairs()
    outer = jnp.where(even, head, tail)
    outer = jnp.where(pole, jnp.flip(outer, 0), outer)
    got_first = lax.ppermute(jnp.where(even, tail, head), AXES, first)
    got_second = lax.ppermute(outer, AXES, second)
    return got_first, got_second


def body(state_field, cotangent, depthwise, norm_gain, w_in, w_out):
    grad_scale = 1.0 / math.sqrt(CELLS * LAT * LON)
    lat, lon = lat_lon()
    lat = lat.astype(jnp.int32)
    west = (lon % 2 == 0).astype(jnp.int32)
    even = lat % 2 == 0
    pole = (lat == 0) | (lat == LAT - 1)
    parity = even.astype(jnp.int32)
    core = jnp.stack([lax.axis_index("core").astype(jnp.int32), west])
    cot = cotangent.reshape(CELLS, C)
    gain = norm_gain.reshape(1, C)
    *own_edges, gain, w_in, w_out = call(
        own_edge_kernel,
        [
            ((9 * H, C), F32),
            ((9 * H, C), F32),
            ((1, C), F32),
            ((C, FF), BF16),
            ((FF, C), BF16),
        ],
        state_field, cot, gain, w_in, w_out,
        scratch=[
            ((H, W, C), F32),
            ((CELLS, C), BF16),
            ((CELLS, C), F32),
            pltpu.SemaphoreType.DMA((5,)),
        ],
        held=(0, 1, 2, 3, 4),
    )
    rows = row_exchange(state_field, even, pole)
    above, below, to_near, to_far = call(
        edge_kernel,
        [((3, W, C), F32), ((3, W, C), F32), ((EDGE, C), F32), ((EDGE, C), F32)],
        jnp.stack([parity, west]), *rows, *own_edges,
        scalars=1,
    )
    near, far = column_pairs()
    near = lax.ppermute(to_near, AXES, near)
    far = lax.ppermute(to_far, AXES, far)
    part = ((16, 128, 128), F32)
    mine, theirs, middle, grad_middle, tap_middle = call(
        middle_kernel,
        [part, part, ((HALF_CELLS, FF), BF16), ((H, M, C), F32), ((128, 128), F32)],
        core, above, below, state_field, cot, depthwise, gain, w_in, w_out,
        scratch=[
            ((H + 6, W, C), F32),
            ((HALF_CELLS, C), F32),
            ((H, W, C), F32),
            ((HALF_CELLS, FF), BF16),
        ],
        scalars=1,
    )
    mine, theirs, hidden, grad_pre, centred, inv_std, before, after = call(
        forward_kernel,
        [
            part,
            part,
            ((HALF_CELLS, FF), BF16),
            ((HALF_CELLS, FF), BF16),
            ((HALF_CELLS, C), F32),
            ((HALF_CELLS, 128), F32),
            ((EDGE, C), F32),
            ((EDGE, C), F32),
        ],
        core, above, below, state_field, near, far, cot, depthwise, gain, w_in, w_out, mine, theirs,
        scratch=[WIDE, ((HALF_CELLS, C), F32), ((H, M, C), F32)],
        scalars=1,
    )
    theirs = lax.ppermute(theirs, "core", [(0, 1), (1, 0)])
    grad_conv, taps = call(
        backward_kernel,
        [((H, V, C), F32), ((128, 128), F32)],
        above, below, state_field, before, after, gain, w_in, grad_pre, centred, inv_std, grad_middle, tap_middle,
        scratch=[WIDE, ((H, M, C), F32)],
    )
    (joined,) = call(join_kernel, [((16, 136, 128), F32)], mine, theirs, taps)
    plane = lax.all_to_all(joined, ("x", "y"), split_axis=0, concat_axis=0, tiled=True)
    grad_rows = row_exchange(grad_conv, even, pole)
    plane, grad_rows = lax.optimization_barrier((plane, grad_rows))
    (spread,) = call(plane_kernel, [((16, 16, 128), F32)], plane)
    column = lax.all_to_all(spread, ("zh", "zl"), split_axis=0, concat_axis=0, tiled=True)
    grad_input, block_out = call(
        adjoint_kernel,
        [((CELLS, C), BF16), ((CELLS, C), BF16)],
        jnp.stack([lat, parity]), *grad_rows, grad_conv, cot, depthwise, state_field, middle, hidden, w_out,
        scratch=[
            ((H + 6, V, C), F32),
            ((2, 7, 8, C), F32),
            ((CELLS, C), F32),
            ((H, V, C), F32),
        ],
        scalars=1,
    )
    column, grad_input = lax.optimization_barrier((column, grad_input))
    weight_grads, shared = call(
        functools.partial(column_kernel, grad_scale), [((2, 512), F32), ((32, 8, 128), F32)], column
    )
    shared = lax.all_to_all(shared, ("x", "core", "y"), split_axis=0, concat_axis=0, tiled=True)
    tap_total, gain_total = call(total_kernel, [((49, C), F32), ((1, C), F32)], shared)
    return (
        block_out.reshape(H, W, C),
        grad_input.reshape(H, W, C),
        weight_grads,
        tap_total,
        gain_total.reshape(C),
    )


def solution(mesh):
    split = Mesh(mesh.devices.reshape(SIZES), AXES)
    cells = P(("zh", "x", "core"), ("y", "zl"), None)
    return jax.shard_map(
        body,
        mesh=split,
        in_specs=(cells, cells, P(), P(), P(), P()),
        out_specs=(cells, cells, P(AXES, None), P(), P()),
        check_vma=False,
    )
```
